128 devices in a mesh: dp: 2 (over z_lo), ctx: 8 (over x, core), tensor: 8 (over z_hi, y).
Axes of the slice: x: 4, y: 4, z: 4 (z_hi: 2, z_lo: 2; z = z_hi * 2 + z_lo), core: 2. Of those that a mesh axis runs over, the one named last changes fastest.
Arguments:
- tokens: bfloat16 [8192, 8192], P(('dp', 'ctx'), 'tensor'), may hold values from -6 to 6
- norm_gain: float32 [8192], replicated, may hold values from 0.5 to 14
- project_weight: bfloat16 [8192, 8, 768], P(None, 'tensor'), may hold values from -0.0625 to 0.0625
- project_bias: bfloat16 [8, 768], P('tensor'), may hold values from -3 to 3
- output_weight: bfloat16 [4096, 8192], P('tensor'), may hold values from -0.09375 to 0.09375
- source_row: int32 [8192], P(('dp', 'ctx')), may hold values from 0 to 8191, as said below
- segment_id: int32 [8192], P(('dp', 'ctx')), may hold values from 0 to 11, as said below
Outputs:
- sublayer_out: bfloat16 [8192, 8192], P(('dp', 'ctx', 'tensor'))
The draws below stay inside these ranges and needn't reach their ends.
Inputs may be any that keep to these rules, and one draw needn't show every extreme that they name: `source_row`: A permutation of the rollout rows; each document moves as one run in its order. `segment_id`: each packed sequence of 4096 positions holds exactly 6 documents, each a run of equal ids; ids differ between packed sequences.
All inputs are finite; a program needn't handle non-finite values.
Results may differ from the reference program's by a relative error of at most 0.023.
The reference program's roundings to bfloat16 on the way count: a program that leaves them out, or rounds other values in their place, can miss the bound.
Values may be sent and summed in bfloat16 or wider, within the bound.
A program may use at most 128 MiB of HBM per device.

```python
import jax
import jax.numpy as jnp
from jax import lax

D = 8192
HEADS_KV = 8
HD = 128
GROUP = 4
DOCS = 6
PACK = 4096
TOKENS = 8192
N_TENSOR = 8


def packing(key):
    pack_count = TOKENS // PACK
    shortest = PACK // (4 * DOCS)
    free_room = PACK - DOCS * shortest
    key_list = jax.random.split(key, pack_count + 1)

    def cuts_of(pack_key):
        chosen = jax.random.permutation(pack_key, free_room)[:DOCS - 1] + 1
        chosen = jnp.sort(chosen)
        return (chosen + jnp.arange(1, DOCS) * shortest).astype(jnp.int32)
    cut_points = jax.vmap(cuts_of)(key_list[:pack_count])
    bounds = jnp.concatenate([jnp.zeros((pack_count, 1), jnp.int32), cut_points, jnp.full((pack_count, 1), PACK, jnp.int32)], axis=1)
    doc_lengths = (bounds[:, 1:] - bounds[:, :-1]).reshape(-1)
    place_index = jnp.arange(PACK, dtype=jnp.int32)
    local_doc = jnp.sum((place_index[None, :, None] >= cut_points[:, None, :]).astype(jnp.int32), axis=-1)
    segments = local_doc + jnp.arange(pack_count, dtype=jnp.int32)[:, None] * DOCS
    doc_order = jax.random.permutation(key_list[pack_count], pack_count * DOCS)
    moved_lengths = doc_lengths[doc_order]
    offsets = jnp.cumsum(moved_lengths) - moved_lengths
    rollout_start = jnp.zeros((pack_count * DOCS,), jnp.int32).at[doc_order].set(offsets.astype(jnp.int32))
    doc_start = bounds[:, :DOCS].reshape(-1)
    source_rows = rollout_start[segments] + (place_index[None, :] - doc_start[segments])
    return (source_rows.reshape(-1).astype(jnp.int32), segments.reshape(-1).astype(jnp.int32))


def draw_source_row(key, part):
    return packing(key)[0]


def draw_segment_id(key, part):
    return packing(key)[1]


def draw_norm_gain(key, part):
    key = jax.random.fold_in(key, 11)
    return jax.random.uniform(key, (D,), jnp.float32, 0.5, 1.5)


def shard_levels(own_key, dims, pieces, low, top_value):
    loudness = 1.0
    for position, parts in pieces:
        steps = jax.random.uniform(jax.random.fold_in(jax.random.fold_in(own_key, 6), position), (parts,), jnp.float32, low / len(pieces), top_value / len(pieces))
        loudness = loudness * jnp.repeat(jnp.exp(steps), dims[position] // parts).reshape((-1,) + (1,) * (len(dims) - 1 - position))
    return loudness


def centred(own_key, shape, spread, most, cuts=(), held_as=jnp.bfloat16):
    entries = spread * jax.random.normal(own_key, shape, jnp.float32)
    if cuts:
        entries = entries * shard_levels(own_key, shape, cuts, -0.22, 0.18)
    return jnp.clip(entries, -most, most).astype(held_as)


def setup_inputs(seed: int = 0) -> dict:
    streams_of = jax.random.split(jax.random.key(seed), 8)
    tokens = centred(streams_of[0], (TOKENS, D), 1.0, 6.0, ((0, 16), (1, 8)))
    norm_gain = draw_norm_gain(jax.random.fold_in(streams_of[7], 71), 0)
    project_weight = centred(streams_of[2], (D, HEADS_KV, (GROUP + 2) * HD), D ** -0.5, 0.0625, ((1, 8),))
    project_bias = centred(streams_of[3], (HEADS_KV, (GROUP + 2) * HD), 0.5, 3.0, ((0, 8),))
    output_weight = centred(streams_of[4], (HEADS_KV * GROUP * HD, D), (HEADS_KV * GROUP * HD) ** -0.5, 0.09375, ((0, 8),))
    source_row = draw_source_row(jax.random.fold_in(streams_of[7], 71), 0)
    segment_id = draw_segment_id(jax.random.fold_in(streams_of[7], 71), 0)
    return {"tokens": tokens, "norm_gain": norm_gain, "project_weight": project_weight, "project_bias": project_bias, "output_weight": output_weight, "source_row": source_row, "segment_id": segment_id}


def angle_tables(positions):
    half_size = HD // 2
    freqs = 1000000.0 ** (-(jnp.arange(half_size, dtype=jnp.float32) * 2.0) / HD)
    angles = positions.astype(jnp.float32)[:, None] * freqs[None, :]
    return (jnp.cos(angles), jnp.sin(angles))

def rotate_pairs(values, cosine, sine_part):
    half_size = HD // 2
    first_half = values[..., :half_size]
    second_half = values[..., half_size:]
    return jnp.concatenate([first_half * cosine - second_half * sine_part, second_half * cosine + first_half * sine_part], axis=-1)

def reference(tokens, norm_gain, project_weight, project_bias, output_weight, source_row, segment_id):
    packed = tokens[source_row]
    wide = packed.astype(jnp.float32)
    meansq = lax.optimization_barrier(jnp.mean(wide * wide, axis=-1, keepdims=True))
    normed = (wide * lax.rsqrt(meansq + 1e-06) * norm_gain.astype(jnp.float32)).astype(jnp.bfloat16)
    flat_weight = project_weight.reshape(D, -1)
    projected = (jnp.dot(normed, flat_weight, preferred_element_type=jnp.float32) + project_bias.reshape(-1).astype(jnp.float32)).astype(jnp.bfloat16)
    stacked = lax.optimization_barrier(projected).astype(jnp.float32).reshape(TOKENS, HEADS_KV, GROUP + 2, HD)
    positions = jnp.arange(TOKENS, dtype=jnp.int32) % PACK
    cosine, sine_part = angle_tables(positions)
    queries = rotate_pairs(stacked[:, :, :GROUP], cosine[:, None, None], sine_part[:, None, None]).astype(jnp.bfloat16)
    keys_rot = rotate_pairs(stacked[:, :, GROUP], cosine[:, None], sine_part[:, None]).astype(jnp.bfloat16)
    values = stacked[:, :, GROUP + 1]
    pack_count = TOKENS // PACK
    query_heads = queries.reshape(pack_count, PACK, HEADS_KV, GROUP, HD).transpose(0, 2, 3, 1, 4).reshape(-1, PACK, HD)
    key_heads = jnp.broadcast_to(keys_rot.reshape(pack_count, PACK, HEADS_KV, 1, HD).transpose(0, 2, 3, 1, 4), (pack_count, HEADS_KV, GROUP, PACK, HD)).reshape(-1, PACK, HD)
    value_heads = jnp.broadcast_to(values.reshape(pack_count, PACK, HEADS_KV, 1, HD).transpose(0, 2, 3, 1, 4), (pack_count, HEADS_KV, GROUP, PACK, HD)).reshape(-1, PACK, HD)
    segment_heads = jnp.broadcast_to(segment_id.reshape(pack_count, 1, 1, PACK), (pack_count, HEADS_KV, GROUP, PACK)).reshape(-1, PACK)
    place_index = jnp.arange(PACK, dtype=jnp.int32)
    causal = place_index[None, :] <= place_index[:, None]

    def one_head(operands):
        query_block, key_block, value_block, segments = operands
        scores = jnp.dot(query_block, key_block.T, preferred_element_type=jnp.float32) * HD ** (-0.5)
        allowed = causal & (segments[:, None] == segments[None, :])
        scores = jnp.where(allowed, scores, -1e+30)
        row_max = lax.optimization_barrier(jnp.max(scores, axis=-1, keepdims=True))
        weights = jnp.where(allowed, jnp.exp(scores - row_max), 0.0)
        weighted = jnp.dot(weights, value_block, precision=lax.Precision.HIGHEST)
        return weighted / lax.optimization_barrier(jnp.sum(weights, axis=-1, keepdims=True))
    attended = lax.map(one_head, (query_heads, key_heads, value_heads, segment_heads))
    attended = attended.reshape(pack_count, HEADS_KV, GROUP, PACK, HD).transpose(0, 3, 1, 2, 4).reshape(TOKENS, -1).astype(jnp.bfloat16)
    unpacked = jnp.zeros_like(attended).at[source_row].set(attended)
    block_cols = attended.shape[1] // N_TENSOR
    summed = jnp.zeros((TOKENS, D), jnp.float32)
    for portion in range(N_TENSOR):
        partial_term = jnp.dot(unpacked[:, portion * block_cols:(portion + 1) * block_cols], output_weight[portion * block_cols:(portion + 1) * block_cols], preferred_element_type=jnp.float32).astype(jnp.bfloat16)
        summed = summed + lax.optimization_barrier(partial_term).astype(jnp.float32)
    return summed.astype(jnp.bfloat16)
```

```python
import functools

import jax
import jax.numpy as jnp
from jax import lax
from jax.experimental import pallas as pl
from jax.experimental.pallas import tpu as pltpu
from jax.sharding import PartitionSpec as P

HD = 128
GROUP = 4
PACK = 4096
DOC_IDS = 12
N_T = 8
SUBS = 4
MESH = pl.DeviceIdType.MESH
VMEM = pltpu.VMEM
DMA = pltpu.SemaphoreType.DMA


def peer(index):
    return {"tensor": index}


def greet(others):
    barrier = pltpu.get_barrier_semaphore()
    for other in others:
        pl.semaphore_signal(barrier, inc=1, device_id=peer(other), device_id_type=MESH)


def greeted(count):
    pl.semaphore_wait(pltpu.get_barrier_semaphore(), count)


def remote(src, dst, send_sem, recv_sem, to):
    return pltpu.make_async_remote_copy(
        src_ref=src,
        dst_ref=dst,
        send_sem=send_sem,
        recv_sem=recv_sem,
        device_id=peer(to),
        device_id_type=MESH,
    )


def all_others(me):
    return [lax.rem(me + d, N_T) for d in range(1, N_T)]


def norm_kernel(
    features,
    tok_ref,
    gain_ref,
    wo_ref,
    normed_ref,
    shuffled_ref,
    stats,
    stat_send,
    stat_recv,
    w_send,
    w_recv,
    own_sem,
):
    me = lax.axis_index("tensor")
    replica = lax.axis_index("dp") * lax.axis_size("ctx") + lax.axis_index("ctx")
    rows, width = tok_ref.shape
    piece, columns = shuffled_ref.shape[1:]
    others = all_others(me)
    greet(others)
    block = 128
    for i in range(rows // block):
        total = jnp.zeros((block, 128), jnp.float32)
        for j in range(width // 128):
            part = tok_ref[i * block : (i + 1) * block, j * 128 : (j + 1) * 128].astype(jnp.float32)
            total = total + part * part
        summed = jnp.sum(total.T, axis=0, keepdims=True)
        stats[pl.ds(me, 1), :, i * block : (i + 1) * block] = jnp.broadcast_to(
            summed[None], (1, 8, block)
        )
    greeted(N_T - 1)
    mine = pl.ds(pl.multiple_of(replica * piece, piece), piece)

    def columns_of(index):
        return pl.ds(pl.multiple_of(index * columns, columns), columns)

    stat_copies = []
    w_copies = []
    for d, other in enumerate(others):
        copy = remote(
            stats.at[me], stats.at[me], stat_send.at[d], stat_recv.at[d], other
        )
        copy.start()
        stat_copies.append(copy)
    for d, other in enumerate(others):
        copy = remote(
            wo_ref.at[mine, columns_of(other)],
            shuffled_ref.at[me],
            w_send.at[d],
            w_recv.at[d],
            other,
        )
        copy.start()
        w_copies.append(copy)
    own = pltpu.make_async_copy(wo_ref.at[mine, columns_of(me)], shuffled_ref.at[me], own_sem)
    own.start()
    for copy in stat_copies:
        copy.wait()
    summed = stats[0]
    for t in range(1, N_T):
        summed = summed + stats[t]
    scale = lax.rsqrt(summed[0:1] * (1.0 / features) + 1e-06)
    for i in range(rows // block):
        along = jnp.broadcast_to(scale[:, i * block : (i + 1) * block], (128, block)).T
        for j in range(width // 128):
            cut = (slice(i * block, (i + 1) * block), slice(j * 128, (j + 1) * 128))
            gain = gain_ref[me, :, j * 128 : (j + 1) * 128]
            normed_ref[cut] = (tok_ref[cut].astype(jnp.float32) * along * gain).astype(jnp.bfloat16)
    own.wait()
    for copy in w_copies:
        copy.wait()


def normalise(tokens, gain, out_weight, replicas):
    rows, width = tokens.shape
    depth, out_width = out_weight.shape
    piece, columns = depth // replicas, out_width // N_T
    return pl.pallas_call(
        functools.partial(norm_kernel, width * N_T),
        out_shape=(
            jax.ShapeDtypeStruct((rows, width), jnp.bfloat16),
            jax.ShapeDtypeStruct((N_T, piece, columns), jnp.bfloat16),
        ),
        in_specs=[
            pl.BlockSpec(memory_space=VMEM),
            pl.BlockSpec(memory_space=VMEM),
            pl.BlockSpec(memory_space=pl.ANY),
        ],
        out_specs=(pl.BlockSpec(memory_space=VMEM), pl.BlockSpec(memory_space=pl.ANY)),
        scratch_shapes=[
            VMEM((N_T, 8, rows), jnp.float32),
            DMA((N_T - 1,)),
            DMA((N_T - 1,)),
            DMA((N_T - 1,)),
            DMA((N_T - 1,)),
            DMA,
        ],
        compiler_params=pltpu.CompilerParams(
            collective_id=1, has_side_effects=True, vmem_limit_bytes=32 * 2**20
        ),
        cost_estimate=pl.CostEstimate(flops=10**7, bytes_accessed=10**7, transcendentals=0),
    )(tokens, gain.reshape(N_T, 1, width), out_weight)


class Gather:
    def __init__(self, own_ref, buf, send_sem, recv_sem):
        me = lax.axis_index("tensor")
        y = lax.rem(me, 4)
        base = me - y
        self.me = me
        self.own_ref, self.buf, self.send_sem, self.recv_sem = own_ref, buf, send_sem, recv_sem
        self.up = base + lax.rem(y + 1, 4)
        self.down = base + lax.rem(y + 3, 4)
        far = base + lax.rem(y + 2, 4)

        def across(t):
            return lax.rem(t + 4, N_T)

        self.pair = across(me)
        self.owner = [
            self.down,
            self.up,
            self.pair,
            far,
            across(self.down),
            across(self.up),
            across(far),
        ]
        self.step = own_ref.shape[0] // SUBS
        self.started = []

    def greet(self):
        greet([self.up, self.down, self.pair])

    def greeted(self):
        greeted(3)

    def rows(self, s):
        return pl.ds(s * self.step, self.step)

    def send(self, src, owner, kind, s, to):
        copy = remote(
            src.at[self.rows(s)],
            self.buf.at[owner, self.rows(s)],
            self.send_sem.at[len(self.started)],
            self.recv_sem.at[kind, s],
            to,
        )
        copy.start()
        self.started.append(copy)

    def forward(self, owner, kind, s, to):
        self.send(self.buf.at[owner], owner, kind, s, to)

    def wait(self, kind, s):
        owner = self.owner[kind]
        place = self.buf.at[owner, self.rows(s)]
        remote(place, place, self.send_sem.at[0], self.recv_sem.at[kind, s], self.pair).wait_recv()

    def send_own(self):
        for s in range(SUBS):
            self.send(self.own_ref, self.me, 2, s, self.pair)
            self.send(self.own_ref, self.me, 0, s, self.up)
            self.send(self.own_ref, self.me, 1, s, self.down)

    def run(self, use):
        half = SUBS // 2
        self.send_own()
        use(self.own_ref, self.me)
        for s in range(SUBS):
            self.wait(0, s)
            if s < half:
                self.forward(self.owner[0], 3, s, self.up)
            self.wait(1, s)
            if s >= half:
                self.forward(self.owner[1], 3, s, self.down)
            self.wait(2, s)
            self.forward(self.pair, 4, s, self.up)
            self.forward(self.pair, 5, s, self.down)
        for kind in range(3):
            use(self.buf.at[self.owner[kind]], self.owner[kind])
        for s in range(SUBS):
            self.wait(4, s)
            if s < half:
                self.forward(self.owner[4], 6, s, self.up)
            self.wait(5, s)
            if s >= half:
                self.forward(self.owner[5], 6, s, self.down)
        for s in range(SUBS):
            self.wait(3, s)
        for kind in (3, 4, 5):
            use(self.buf.at[self.owner[kind]], self.owner[kind])
        for s in range(SUBS):
            self.wait(6, s)
        use(self.buf.at[self.owner[6]], self.owner[6])
        for copy in self.started:
            copy.wait_send()


GATHER_SENDS = 7 * SUBS
GATHER_SEMS = [DMA((GATHER_SENDS,)), DMA((7, SUBS))]


def project_kernel(own_ref, w_ref, bias_ref, out_ref, buf, w_buf, total, send_sem, recv_sem, w_sem):
    width = own_ref.shape[1]
    gather = Gather(own_ref, buf, send_sem, recv_sem)
    gather.greet()
    order = [gather.me] + gather.owner
    loads = []
    for i, t in enumerate(order):
        load = pltpu.make_async_copy(
            w_ref.at[pl.ds(pl.multiple_of(t * width, width), width)], w_buf.at[i], w_sem.at[i]
        )
        load.start()
        loads.append(load)
    gather.greeted()
    used = []

    def use(chunk, owner):
        i = len(used)
        used.append(owner)
        loads[i].wait()
        tile = min(256, total.shape[1])

        def one(n, _):
            cut = pl.ds(pl.multiple_of(n * tile, tile), tile)
            term = jnp.dot(chunk[...], w_buf[i, :, cut], preferred_element_type=jnp.float32)
            if i == 0:
                total[:, cut] = term
            else:
                total[:, cut] += term
            return 0

        lax.fori_loop(0, total.shape[1] // tile, one, 0)

    gather.run(use)
    bias = bias_ref[...].astype(jnp.float32)
    out_ref[...] = (total[...] + bias).astype(jnp.bfloat16)


def project(normed, weight, bias):
    rows, width = normed.shape
    columns = weight.shape[1]
    return pl.pallas_call(
        project_kernel,
        out_shape=jax.ShapeDtypeStruct((rows, columns), jnp.bfloat16),
        in_specs=[
            pl.BlockSpec(memory_space=VMEM),
            pl.BlockSpec(memory_space=pl.ANY),
            pl.BlockSpec(memory_space=VMEM),
        ],
        out_specs=pl.BlockSpec(memory_space=VMEM),
        scratch_shapes=[
            VMEM((N_T, rows, width), jnp.bfloat16),
            VMEM((N_T, width, columns), jnp.bfloat16),
            VMEM((rows, columns), jnp.float32),
            *GATHER_SEMS,
            DMA((N_T,)),
        ],
        compiler_params=pltpu.CompilerParams(
            collective_id=2, has_side_effects=True, vmem_limit_bytes=48 * 2**20
        ),
        cost_estimate=pl.CostEstimate(
            flops=2 * rows * width * N_T * columns,
            bytes_accessed=10**8,
            transcendentals=0,
        ),
    )(normed, weight, bias)


def output_kernel(
    own_ref, w_ref, out_ref, buf, w_buf, total, done, send_sem, recv_sem, w_sem, out_send, out_recv, own_sem
):
    me = lax.axis_index("tensor")
    gather = Gather(own_ref, buf, send_sem, recv_sem)
    others = all_others(me)
    greet(others)
    order = [gather.me] + gather.owner
    loads = []
    for i, t in enumerate(order):
        load = pltpu.make_async_copy(w_ref.at[:, t], w_buf.at[i], w_sem.at[i])
        load.start()
        loads.append(load)
    greeted(N_T - 1)
    used = []
    depth = own_ref.shape[1]
    columns = total.shape[1]

    def use(chunk, owner):
        i = len(used)
        used.append(owner)
        loads[i].wait()
        tile = min(256, columns)

        def one(n, _):
            cut = pl.ds(pl.multiple_of(n * tile, tile), tile)
            weight = w_buf[i, :, :, cut].reshape(depth, tile)
            term = jnp.dot(chunk[...], weight, preferred_element_type=jnp.float32)
            term = term.astype(jnp.bfloat16).astype(jnp.float32)
            if i == 0:
                total[:, cut] = term
            else:
                total[:, cut] += term
            return 0

        lax.fori_loop(0, columns // tile, one, 0)

    gather.run(use)
    done[...] = total[...].astype(jnp.bfloat16)
    part = out_ref.shape[0]

    def rows_of(t):
        return pl.ds(pl.multiple_of(t * part, part), part)

    place = out_ref.at[:, pl.ds(pl.multiple_of(me * columns, columns), columns)]
    copies = []
    for d, other in enumerate(others):
        copy = remote(done.at[rows_of(other)], place, out_send.at[d], out_recv.at[d], other)
        copy.start()
        copies.append(copy)
    own = pltpu.make_async_copy(done.at[rows_of(me)], place, own_sem)
    own.start()
    own.wait()
    for copy in copies:
        copy.wait()


def project_out(attended, weight):
    rows, depth = attended.shape
    columns = weight.shape[3]
    return pl.pallas_call(
        output_kernel,
        out_shape=jax.ShapeDtypeStruct((rows // N_T, columns * N_T), jnp.bfloat16),
        in_specs=[pl.BlockSpec(memory_space=VMEM), pl.BlockSpec(memory_space=pl.ANY)],
        out_specs=pl.BlockSpec(memory_space=pl.ANY),
        scratch_shapes=[
            VMEM((N_T, rows, depth), jnp.bfloat16),
            VMEM((N_T, weight.shape[0], weight.shape[2], columns), jnp.bfloat16),
            VMEM((rows, columns), jnp.float32),
            VMEM((rows, columns), jnp.bfloat16),
            *GATHER_SEMS,
            DMA((N_T,)),
            DMA((N_T - 1,)),
            DMA((N_T - 1,)),
            DMA,
        ],
        compiler_params=pltpu.CompilerParams(
            collective_id=3, has_side_effects=True, vmem_limit_bytes=48 * 2**20
        ),
        cost_estimate=pl.CostEstimate(
            flops=2 * rows * depth * N_T * columns, bytes_accessed=10**8, transcendentals=0
        ),
    )(attended, weight)


TILE_Q = 256
TILE_K = 256
LOW = -1e30


def attend_kernel(first_ref, start_ref, q_ref, k_ref, v_ref, out_ref):
    rows = q_ref.shape[0]
    heads = q_ref.shape[1] // HD
    factor = HD**-0.5 * 1.4426950408889634
    for a in range(rows // TILE_Q):
        base = first_ref[0] + a * TILE_Q
        start = start_ref[:, a * TILE_Q : (a + 1) * TILE_Q]
        query_row = base + lax.broadcasted_iota(jnp.int32, (1, TILE_Q), 1)
        low_tile = lax.div(first_ref[1 + a], TILE_K)
        high_tile = lax.div(base + TILE_Q, TILE_K)

        def one(i, carry, a=a, start=start, query_row=query_row, high_tile=high_tile):
            tile = high_tile - 1 - i
            cut = pl.ds(pl.multiple_of(tile * TILE_K, TILE_K), TILE_K)
            keys = k_ref[cut]
            values = v_ref[cut].T
            key_row = tile * TILE_K + lax.broadcasted_iota(jnp.int32, (TILE_K, TILE_Q), 0)
            allowed = (key_row >= start) & (key_row <= query_row)
            after = []
            for h in range(heads):
                top, denominator, weighted = carry[h]
                query = q_ref[a * TILE_Q : (a + 1) * TILE_Q, h * HD : (h + 1) * HD]
                scores = lax.dot_general(
                    keys, query, (((1,), (1,)), ((), ())), preferred_element_type=jnp.float32
                )
                scores = jnp.where(allowed, scores * factor, 2 * LOW)
                new_top = jnp.maximum(top, jnp.max(scores, axis=0, keepdims=True))
                weights = jnp.exp2(scores - new_top)
                shrink = jnp.exp2(top - new_top)
                denominator = denominator * shrink + jnp.sum(weights, axis=0, keepdims=True)
                coarse = weights.astype(jnp.bfloat16)
                fine = (weights - coarse.astype(jnp.float32)).astype(jnp.bfloat16)
                weighted = weighted * shrink
                weighted += jnp.dot(values, coarse, preferred_element_type=jnp.float32)
                weighted += jnp.dot(values, fine, preferred_element_type=jnp.float32)
                after.append((new_top, denominator, weighted))
            return tuple(after)

        begin = (
            jnp.full((1, TILE_Q), LOW, jnp.float32),
            jnp.zeros((1, TILE_Q), jnp.float32),
            jnp.zeros((HD, TILE_Q), jnp.float32),
        )
        ended = lax.fori_loop(0, high_tile - low_tile, one, (begin,) * heads)
        for h in range(heads):
            _, denominator, weighted = ended[h]
            out_ref[a * TILE_Q : (a + 1) * TILE_Q, h * HD : (h + 1) * HD] = (
                (weighted / denominator).T.astype(jnp.bfloat16)
            )


def attend(first_row, start, queries, keys, values):
    rows = queries.shape[0]
    scalars = jnp.concatenate([first_row[None], start[:: TILE_Q]]).astype(jnp.int32)
    vmem = pl.BlockSpec(memory_space=VMEM)
    return pl.pallas_call(
        attend_kernel,
        out_shape=jax.ShapeDtypeStruct(queries.shape, jnp.bfloat16),
        in_specs=[pl.BlockSpec(memory_space=pltpu.SMEM), vmem, vmem, vmem, vmem],
        out_specs=vmem,
        compiler_params=pltpu.CompilerParams(vmem_limit_bytes=40 * 2**20),
        cost_estimate=pl.CostEstimate(flops=10**9, bytes_accessed=10**7, transcendentals=10**7),
    )(scalars, start.reshape(1, rows), queries, keys, values)


def angle_tables(positions):
    half_size = HD // 2
    freqs = 1000000.0 ** (-(jnp.arange(half_size, dtype=jnp.float32) * 2.0) / HD)
    angles = positions.astype(jnp.float32)[:, None] * freqs[None, :]
    return (jnp.cos(angles), jnp.sin(angles))


def rotate_pairs(values, cosine, sine_part):
    half_size = HD // 2
    first_half = values[..., :half_size]
    second_half = values[..., half_size:]
    return jnp.concatenate(
        [
            first_half * cosine - second_half * sine_part,
            second_half * cosine + first_half * sine_part,
        ],
        axis=-1,
    )


def document_places(source_row, segment_id, rows):
    both = lax.all_gather(jnp.stack([source_row, segment_id]), ("dp", "ctx"), axis=0)
    sources = both[:, 0].reshape(-1)
    segments = both[:, 1].reshape(-1)
    count = sources.shape[0]
    of_doc = segments[None, :] == jnp.arange(DOC_IDS, dtype=jnp.int32)[:, None]
    rollout_start = jnp.min(jnp.where(of_doc, sources[None, :], count), axis=1)
    packed_start = jnp.min(
        jnp.where(of_doc, jnp.arange(count, dtype=jnp.int32)[None, :], count), axis=1
    )
    begun = rollout_start[None, :] <= rows[:, None]
    start = jnp.max(jnp.where(begun, rollout_start[None, :], 0), axis=1)
    shift = jnp.sum(
        jnp.where(
            begun & (rollout_start[None, :] == start[:, None]),
            (packed_start - rollout_start)[None, :],
            0,
        ),
        axis=1,
    )
    return start, rows + shift


def per_device(
    tokens, norm_gain, project_weight, project_bias, output_weight, source_row, segment_id
):
    local_rows = tokens.shape[0]
    replicas = lax.axis_size("dp") * lax.axis_size("ctx")
    first_row = lax.axis_index(("dp", "ctx")) * local_rows
    rows = first_row + jnp.arange(local_rows, dtype=jnp.int32)
    normed, shuffled = normalise(tokens, norm_gain, output_weight, replicas)
    out_columns = lax.all_gather(shuffled, ("dp", "ctx"), axis=0)
    start, place = document_places(source_row, segment_id, rows)
    projected = project(normed, project_weight.reshape(project_weight.shape[0], -1), project_bias)
    cosine, sine_part = angle_tables(lax.rem(place, PACK))
    stacked = projected.reshape(local_rows, GROUP + 2, HD)
    turned = rotate_pairs(
        stacked[:, : GROUP + 1].astype(jnp.float32), cosine[:, None], sine_part[:, None]
    ).astype(jnp.bfloat16)
    queries = turned[:, :GROUP].reshape(local_rows, GROUP * HD)
    own = jnp.concatenate([turned[:, GROUP], stacked[:, GROUP + 1]], axis=1)
    both = lax.all_gather(own, ("dp", "ctx"), axis=0, tiled=True)
    attended = attend(first_row, start, queries, both[:, :HD], both[:, HD:])
    return project_out(attended, out_columns)


def solution(mesh):
    placed = (
        P(("dp", "ctx"), "tensor"),
        P(),
        P(None, "tensor", None),
        P("tensor", None),
        P("tensor", None),
        P(("dp", "ctx")),
        P(("dp", "ctx")),
    )
    return jax.shard_map(
        per_device,
        mesh=mesh,
        in_specs=placed,
        out_specs=P(("dp", "ctx", "tensor"), None),
        check_vma=False,
    )
```

```python
import functools

import jax
import jax.numpy as jnp
from jax import lax
from jax.experimental import pallas as pl
from jax.experimental.pallas import tpu as pltpu
from jax.sharding import PartitionSpec as P

HD = 128
GROUP = 4
PACK = 4096
DOC_IDS = 12
N_T = 8
SUBS = 4
MESH = pl.DeviceIdType.MESH
VMEM = pltpu.VMEM
DMA = pltpu.SemaphoreType.DMA


def peer(index):
    return {"tensor": index}


def greet(others):
    barrier = pltpu.get_barrier_semaphore()
    for other in others:
        pl.semaphore_signal(barrier, inc=1, device_id=peer(other), device_id_type=MESH)


def greeted(count):
    pl.semaphore_wait(pltpu.get_barrier_semaphore(), count)


def remote(src, dst, send_sem, recv_sem, to):
    return pltpu.make_async_remote_copy(
        src_ref=src,
        dst_ref=dst,
        send_sem=send_sem,
        recv_sem=recv_sem,
        device_id=peer(to),
        device_id_type=MESH,
    )


def all_others(me):
    return [lax.rem(me + d, N_T) for d in range(1, N_T)]


def norm_kernel(
    features,
    tok_ref,
    gain_ref,
    wo_ref,
    places_ref,
    normed_ref,
    shuffled_ref,
    spots_ref,
    stats,
    docs,
    stat_send,
    stat_recv,
    w_send,
    w_recv,
    doc_send,
    doc_recv,
    own_sem,
):
    me = lax.axis_index("tensor")
    replica = lax.axis_index("dp") * lax.axis_size("ctx") + lax.axis_index("ctx")
    replicas = docs.shape[0]
    rows, width = tok_ref.shape
    piece, columns = shuffled_ref.shape[1:]
    others = all_others(me)
    greet(others)
    alike = [ring_of(lax.rem(replica + d, replicas)) for d in range(1, replicas)]
    for other in alike:
        pl.semaphore_signal(
            pltpu.get_barrier_semaphore(), inc=1, device_id=other, device_id_type=MESH
        )
    sources = places_ref[0:1]
    segments = places_ref[1:2]
    packed_row = replica * rows + lax.broadcasted_iota(jnp.int32, (1, rows), 1)
    none = rows * replicas
    lane = lax.broadcasted_iota(jnp.int32, (8, 128), 1)
    line = lax.broadcasted_iota(jnp.int32, (8, 128), 0)
    table = jnp.full((8, 128), none, jnp.int32)
    for doc in range(DOC_IDS):
        of_doc = segments == doc
        first_source = jnp.min(jnp.where(of_doc, sources, none), axis=1, keepdims=True)
        first_packed = jnp.min(jnp.where(of_doc, packed_row, none), axis=1, keepdims=True)
        found = jnp.where(line == 0, first_source, first_packed)
        table = jnp.where(lane == doc, found, table)
    docs[pl.ds(replica, 1)] = table[None]
    block = 128
    for i in range(rows // block):
        total = jnp.zeros((block, 128), jnp.float32)
        for j in range(width // 128):
            part = tok_ref[i * block : (i + 1) * block, j * 128 : (j + 1) * 128].astype(jnp.float32)
            total = total + part * part
        summed = jnp.sum(total.T, axis=0, keepdims=True)
        stats[pl.ds(me, 1), :, i * block : (i + 1) * block] = jnp.broadcast_to(
            summed[None], (1, 8, block)
        )
    greeted(N_T - 1 + replicas - 1)
    mine = pl.ds(pl.multiple_of(replica * piece, piece), piece)

    def columns_of(index):
        return pl.ds(pl.multiple_of(index * columns, columns), columns)

    stat_copies = []
    w_copies = []
    for d, other in enumerate(others):
        copy = remote(
            stats.at[me], stats.at[me], stat_send.at[d], stat_recv.at[d], other
        )
        copy.start()
        stat_copies.append(copy)
    doc_copies = []
    for d, other in enumerate(alike):
        copy = pltpu.make_async_remote_copy(
            src_ref=docs.at[replica],
            dst_ref=docs.at[replica],
            send_sem=doc_send.at[d],
            recv_sem=doc_recv.at[d],
            device_id=other,
            device_id_type=MESH,
        )
        copy.start()
        doc_copies.append(copy)
    for d, other in enumerate(others):
        copy = remote(
            wo_ref.at[mine, columns_of(other)],
            shuffled_ref.at[me],
            w_send.at[d],
            w_recv.at[d],
            other,
        )
        copy.start()
        w_copies.append(copy)
    own = pltpu.make_async_copy(wo_ref.at[mine, columns_of(me)], shuffled_ref.at[me], own_sem)
    own.start()
    for copy in stat_copies:
        copy.wait()
    summed = stats[0]
    for t in range(1, N_T):
        summed = summed + stats[t]
    scale = lax.rsqrt(summed[0:1] * (1.0 / features) + 1e-06)
    for i in range(rows // block):
        along = jnp.broadcast_to(scale[:, i * block : (i + 1) * block], (128, block)).T
        for j in range(width // 128):
            cut = (slice(i * block, (i + 1) * block), slice(j * 128, (j + 1) * 128))
            gain = gain_ref[me, :, j * 128 : (j + 1) * 128]
            normed_ref[cut] = (tok_ref[cut].astype(jnp.float32) * along * gain).astype(jnp.bfloat16)
    for copy in doc_copies:
        copy.wait()
    table = docs[0]
    for r in range(1, replicas):
        table = jnp.minimum(table, docs[r])
    row = replica * rows + lax.broadcasted_iota(jnp.int32, (1, rows), 1)
    start = jnp.full((1, rows), -1, jnp.int32)
    place = row
    for doc in range(DOC_IDS):
        first_source = table[0:1, doc : doc + 1]
        first_packed = table[1:2, doc : doc + 1]
        later = (first_source <= row) & (first_source > start)
        start = jnp.where(later, first_source, start)
        place = jnp.where(later, row + (first_packed - first_source), place)
    spots_ref[...] = jnp.where(
        lax.broadcasted_iota(jnp.int32, (8, rows), 0) == 0, start, place
    )
    own.wait()
    for copy in w_copies:
        copy.wait()


def ring_of(replica):
    per = lax.axis_size("ctx")
    return {"dp": lax.div(replica, per), "ctx": lax.rem(replica, per)}


def normalise(tokens, gain, out_weight, places, replicas):
    rows, width = tokens.shape
    depth, out_width = out_weight.shape
    piece, columns = depth // replicas, out_width // N_T
    return pl.pallas_call(
        functools.partial(norm_kernel, width * N_T),
        out_shape=(
            jax.ShapeDtypeStruct((rows, width), jnp.bfloat16),
            jax.ShapeDtypeStruct((N_T, piece, columns), jnp.bfloat16),
            jax.ShapeDtypeStruct((8, rows), jnp.int32),
        ),
        in_specs=[
            pl.BlockSpec(memory_space=VMEM),
            pl.BlockSpec(memory_space=VMEM),
            pl.BlockSpec(memory_space=pltpu.HBM),
            pl.BlockSpec(memory_space=VMEM),
        ],
        out_specs=(
            pl.BlockSpec(memory_space=VMEM),
            pl.BlockSpec(memory_space=pltpu.HBM),
            pl.BlockSpec(memory_space=VMEM),
        ),
        scratch_shapes=[
            VMEM((N_T, 8, rows), jnp.float32),
            VMEM((replicas, 8, 128), jnp.int32),
            DMA((N_T - 1,)),
            DMA((N_T - 1,)),
            DMA((N_T - 1,)),
            DMA((N_T - 1,)),
            DMA((replicas - 1,)),
            DMA((replicas - 1,)),
            DMA,
        ],
        compiler_params=pltpu.CompilerParams(
            collective_id=1, has_side_effects=True, vmem_limit_bytes=58 * 2**20
        ),
        cost_estimate=pl.CostEstimate(flops=10**7, bytes_accessed=10**7, transcendentals=0),
    )(tokens, gain.reshape(N_T, 1, width), out_weight, places)


class Gather:
    def __init__(self, own_ref, buf, send_sem, recv_sem):
        me = lax.axis_index("tensor")
        y = lax.rem(me, 4)
        base = me - y
        self.me = me
        self.own_ref, self.buf, self.send_sem, self.recv_sem = own_ref, buf, send_sem, recv_sem
        self.up = base + lax.rem(y + 1, 4)
        self.down = base + lax.rem(y + 3, 4)
        far = base + lax.rem(y + 2, 4)

        def across(t):
            return lax.rem(t + 4, N_T)

        self.pair = across(me)
        self.owner = [
            self.down,
            self.up,
            self.pair,
            far,
            across(self.down),
            across(self.up),
            across(far),
        ]
        self.step = own_ref.shape[0] // SUBS
        self.started = []

    def greet(self):
        greet([self.up, self.down, self.pair])

    def greeted(self):
        greeted(3)

    def rows(self, s):
        return pl.ds(s * self.step, self.step)

    def send(self, src, owner, kind, s, to):
        copy = remote(
            src.at[self.rows(s)],
            self.buf.at[owner, self.rows(s)],
            self.send_sem.at[len(self.started)],
            self.recv_sem.at[kind, s],
            to,
        )
        copy.start()
        self.started.append(copy)

    def forward(self, owner, kind, s, to):
        self.send(self.buf.at[owner], owner, kind, s, to)

    def wait(self, kind, s):
        owner = self.owner[kind]
        place = self.buf.at[owner, self.rows(s)]
        remote(place, place, self.send_sem.at[0], self.recv_sem.at[kind, s], self.pair).wait_recv()

    def send_own(self):
        for s in range(SUBS):
            self.send(self.own_ref, self.me, 2, s, self.pair)
            self.send(self.own_ref, self.me, 0, s, self.up)
            self.send(self.own_ref, self.me, 1, s, self.down)

    def run(self, use):
        half = SUBS // 2
        self.send_own()
        use(self.own_ref, self.me)
        for s in range(SUBS):
            self.wait(0, s)
            if s < half:
                self.forward(self.owner[0], 3, s, self.up)
            self.wait(1, s)
            if s >= half:
                self.forward(self.owner[1], 3, s, self.down)
            self.wait(2, s)
            self.forward(self.pair, 4, s, self.up)
            self.forward(self.pair, 5, s, self.down)
        for kind in range(3):
            use(self.buf.at[self.owner[kind]], self.owner[kind])
        for s in range(SUBS):
            self.wait(4, s)
            if s < half:
                self.forward(self.owner[4], 6, s, self.up)
            self.wait(5, s)
            if s >= half:
                self.forward(self.owner[5], 6, s, self.down)
        for s in range(SUBS):
            self.wait(3, s)
        for kind in (3, 4, 5):
            use(self.buf.at[self.owner[kind]], self.owner[kind])
        for s in range(SUBS):
            self.wait(6, s)
        use(self.buf.at[self.owner[6]], self.owner[6])
        for copy in self.started:
            copy.wait_send()


GATHER_SENDS = 7 * SUBS
GATHER_SEMS = [DMA((GATHER_SENDS,)), DMA((7, SUBS))]


def project_kernel(own_ref, w_ref, bias_ref, out_ref, buf, w_buf, total, send_sem, recv_sem, w_sem):
    width = own_ref.shape[1]
    gather = Gather(own_ref, buf, send_sem, recv_sem)
    gather.greet()
    order = [gather.me] + gather.owner
    loads = []
    for i, t in enumerate(order):
        load = pltpu.make_async_copy(
            w_ref.at[pl.ds(pl.multiple_of(t * width, width), width)], w_buf.at[i], w_sem.at[i]
        )
        load.start()
        loads.append(load)
    gather.greeted()
    used = []

    def use(chunk, owner):
        i = len(used)
        used.append(owner)
        loads[i].wait()
        tile = min(256, total.shape[1])

        def one(n, _):
            cut = pl.ds(pl.multiple_of(n * tile, tile), tile)
            term = jnp.dot(chunk[...], w_buf[i, :, cut], preferred_element_type=jnp.float32)
            if i == 0:
                total[:, cut] = term
            else:
                total[:, cut] += term
            return 0

        lax.fori_loop(0, total.shape[1] // tile, one, 0)

    gather.run(use)
    bias = bias_ref[...].astype(jnp.float32)
    out_ref[...] = (total[...] + bias).astype(jnp.bfloat16)


def project(normed, weight, bias):
    rows, width = normed.shape
    columns = weight.shape[1]
    return pl.pallas_call(
        project_kernel,
        out_shape=jax.ShapeDtypeStruct((rows, columns), jnp.bfloat16),
        in_specs=[
            pl.BlockSpec(memory_space=VMEM),
            pl.BlockSpec(memory_space=pltpu.HBM),
            pl.BlockSpec(memory_space=VMEM),
        ],
        out_specs=pl.BlockSpec(memory_space=VMEM),
        scratch_shapes=[
            VMEM((N_T, rows, width), jnp.bfloat16),
            VMEM((N_T, width, columns), jnp.bfloat16),
            VMEM((rows, columns), jnp.float32),
            *GATHER_SEMS,
            DMA((N_T,)),
        ],
        compiler_params=pltpu.CompilerParams(
            collective_id=2, has_side_effects=True, vmem_limit_bytes=48 * 2**20
        ),
        cost_estimate=pl.CostEstimate(
            flops=2 * rows * width * N_T * columns,
            bytes_accessed=10**8,
            transcendentals=0,
        ),
    )(normed, weight, bias)


def output_kernel(
    own_ref, w_ref, out_ref, buf, w_buf, total, done, send_sem, recv_sem, w_sem, out_send, out_recv, own_sem
):
    me = lax.axis_index("tensor")
    gather = Gather(own_ref, buf, send_sem, recv_sem)
    others = all_others(me)
    greet(others)
    order = [gather.me] + gather.owner
    loads = []
    for i, t in enumerate(order):
        load = pltpu.make_async_copy(w_ref.at[:, t], w_buf.at[i], w_sem.at[i])
        load.start()
        loads.append(load)
    greeted(N_T - 1)
    used = []
    depth = own_ref.shape[1]
    columns = total.shape[1]

    def use(chunk, owner):
        i = len(used)
        used.append(owner)
        loads[i].wait()
        tile = min(256, columns)

        def one(n, _):
            cut = pl.ds(pl.multiple_of(n * tile, tile), tile)
            weight = w_buf[i, :, :, cut].reshape(depth, tile)
            term = jnp.dot(chunk[...], weight, preferred_element_type=jnp.float32)
            term = term.astype(jnp.bfloat16).astype(jnp.float32)
            if i == 0:
                total[:, cut] = term
            else:
                total[:, cut] += term
            return 0

        lax.fori_loop(0, columns // tile, one, 0)

    gather.run(use)
    done[...] = total[...].astype(jnp.bfloat16)
    part = out_ref.shape[0]

    def rows_of(t):
        return pl.ds(pl.multiple_of(t * part, part), part)

    place = out_ref.at[:, pl.ds(pl.multiple_of(me * columns, columns), columns)]
    copies = []
    for d, other in enumerate(others):
        copy = remote(done.at[rows_of(other)], place, out_send.at[d], out_recv.at[d], other)
        copy.start()
        copies.append(copy)
    own = pltpu.make_async_copy(done.at[rows_of(me)], place, own_sem)
    own.start()
    own.wait()
    for copy in copies:
        copy.wait()


def project_out(attended, weight):
    rows, depth = attended.shape
    columns = weight.shape[3]
    return pl.pallas_call(
        output_kernel,
        out_shape=jax.ShapeDtypeStruct((rows // N_T, columns * N_T), jnp.bfloat16),
        in_specs=[pl.BlockSpec(memory_space=VMEM), pl.BlockSpec(memory_space=pltpu.HBM)],
        out_specs=pl.BlockSpec(memory_space=pltpu.HBM),
        scratch_shapes=[
            VMEM((N_T, rows, depth), jnp.bfloat16),
            VMEM((N_T, weight.shape[0], weight.shape[2], columns), jnp.bfloat16),
            VMEM((rows, columns), jnp.float32),
            VMEM((rows, columns), jnp.bfloat16),
            *GATHER_SEMS,
            DMA((N_T,)),
            DMA((N_T - 1,)),
            DMA((N_T - 1,)),
            DMA,
        ],
        compiler_params=pltpu.CompilerParams(
            collective_id=3, has_side_effects=True, vmem_limit_bytes=48 * 2**20
        ),
        cost_estimate=pl.CostEstimate(
            flops=2 * rows * depth * N_T * columns, bytes_accessed=10**8, transcendentals=0
        ),
    )(attended, weight)


TILE_Q = 256
TILE_K = 256
LOW = -1e30


def attend_kernel(first_ref, start_ref, q_ref, kv_ref, out_ref):
    rows = q_ref.shape[0]
    heads = q_ref.shape[1] // HD
    factor = HD**-0.5 * 1.4426950408889634
    for a in range(rows // TILE_Q):
        base = first_ref[0] + a * TILE_Q
        start = start_ref[:, a * TILE_Q : (a + 1) * TILE_Q]
        query_row = base + lax.broadcasted_iota(jnp.int32, (1, TILE_Q), 1)
        low_tile = lax.div(first_ref[1 + a], TILE_K)
        high_tile = lax.div(base + TILE_Q, TILE_K)

        def one(i, carry, a=a, start=start, query_row=query_row, high_tile=high_tile):
            tile = high_tile - 1 - i
            cut = pl.ds(pl.multiple_of(tile * TILE_K, TILE_K), TILE_K)
            keys = kv_ref[cut, :HD]
            values = kv_ref[cut, HD:].T
            key_row = tile * TILE_K + lax.broadcasted_iota(jnp.int32, (TILE_K, TILE_Q), 0)
            allowed = (key_row >= start) & (key_row <= query_row)
            after = []
            for h in range(heads):
                top, denominator, weighted = carry[h]
                query = q_ref[a * TILE_Q : (a + 1) * TILE_Q, h * HD : (h + 1) * HD]
                scores = lax.dot_general(
                    keys, query, (((1,), (1,)), ((), ())), preferred_element_type=jnp.float32
                )
                scores = jnp.where(allowed, scores * factor, 2 * LOW)
                new_top = jnp.maximum(top, jnp.max(scores, axis=0, keepdims=True))
                weights = jnp.exp2(scores - new_top)
                shrink = jnp.exp2(top - new_top)
                denominator = denominator * shrink + jnp.sum(weights, axis=0, keepdims=True)
                coarse = weights.astype(jnp.bfloat16)
                fine = (weights - coarse.astype(jnp.float32)).astype(jnp.bfloat16)
                weighted = weighted * shrink
                weighted += jnp.dot(values, coarse, preferred_element_type=jnp.float32)
                weighted += jnp.dot(values, fine, preferred_element_type=jnp.float32)
                after.append((new_top, denominator, weighted))
            return tuple(after)

        begin = (
            jnp.full((1, TILE_Q), LOW, jnp.float32),
            jnp.zeros((1, TILE_Q), jnp.float32),
            jnp.zeros((HD, TILE_Q), jnp.float32),
        )
        ended = lax.fori_loop(0, high_tile - low_tile, one, (begin,) * heads)
        for h in range(heads):
            _, denominator, weighted = ended[h]
            out_ref[a * TILE_Q : (a + 1) * TILE_Q, h * HD : (h + 1) * HD] = (
                (weighted / denominator).T.astype(jnp.bfloat16)
            )


def attend(first_row, start, queries, both):
    rows = queries.shape[0]
    scalars = jnp.concatenate([first_row[None], start[:: TILE_Q]]).astype(jnp.int32)
    vmem = pl.BlockSpec(memory_space=VMEM)
    return pl.pallas_call(
        attend_kernel,
        out_shape=jax.ShapeDtypeStruct(queries.shape, jnp.bfloat16),
        in_specs=[pl.BlockSpec(memory_space=pltpu.SMEM), vmem, vmem, vmem],
        out_specs=vmem,
        compiler_params=pltpu.CompilerParams(vmem_limit_bytes=40 * 2**20),
        cost_estimate=pl.CostEstimate(flops=10**9, bytes_accessed=10**7, transcendentals=10**7),
    )(scalars, start.reshape(1, rows), queries, both)


def angle_tables(positions):
    half_size = HD // 2
    freqs = 1000000.0 ** (-(jnp.arange(half_size, dtype=jnp.float32) * 2.0) / HD)
    angles = positions.astype(jnp.float32)[:, None] * freqs[None, :]
    return (jnp.cos(angles), jnp.sin(angles))


SEEN_CHIPS = 4


def turn_kernel(proj_ref, cos_ref, sin_ref, q_ref, kv_ref, own, own_sem, send_sem, recv_sem, near_send, near_recv):
    per = lax.axis_size("ctx") // 2
    ctx = lax.axis_index("ctx")
    core = lax.rem(ctx, 2)
    chip = lax.axis_index("dp") * per + lax.div(ctx, 2)
    chips = lax.axis_size("dp") * per
    block = chip * 2 + core
    sibling = {"ctx": ctx + 1 - 2 * core}
    rows = proj_ref.shape[0]

    def same_core(other):
        return {"dp": lax.div(other, per), "ctx": lax.rem(other, per) * 2 + core}

    def signal(other):
        pl.semaphore_signal(
            pltpu.get_barrier_semaphore(), inc=1, device_id=other, device_id_type=MESH
        )

    signal(sibling)
    for k in range(1, chips):
        signal(same_core(lax.rem(chip + k, chips)))

    cosine, sine = cos_ref[...], sin_ref[...]

    def turned(slot):
        wide = proj_ref[:, slot * HD : (slot + 1) * HD].astype(jnp.float32)
        return (wide * cosine + pltpu.roll(wide, HD // 2, 1) * sine).astype(jnp.bfloat16)

    own[:, :HD] = turned(GROUP)
    own[:, HD:] = proj_ref[:, (GROUP + 1) * HD :]

    greeted(chips)

    def to_chip(k):
        return pltpu.make_async_remote_copy(
            src_ref=own,
            dst_ref=kv_ref.at[block],
            send_sem=send_sem.at[k - 1],
            recv_sem=recv_sem.at[k - 1],
            device_id=same_core(chip + k),
            device_id_type=MESH,
        )

    def to_sibling(k):
        place = kv_ref.at[block - 2 * k]
        return pltpu.make_async_remote_copy(
            src_ref=own if k == 0 else place,
            dst_ref=place,
            send_sem=near_send.at[k],
            recv_sem=near_recv.at[k],
            device_id=sibling,
            device_id_type=MESH,
        )

    order = (2, 1, 3, 4)
    for k in order:

        @pl.when(chip + k < chips)
        def _(k=k):
            to_chip(k).start()

    to_sibling(0).start()
    keep = pltpu.make_async_copy(own, kv_ref.at[block], own_sem)
    keep.start()
    for head in range(GROUP):
        q_ref[:, head * HD : (head + 1) * HD] = turned(head)
    for k in (1, 3, 4, 2):

        @pl.when(chip - k >= 0)
        def _(k=k):
            place = kv_ref.at[block - 2 * k]
            pltpu.make_async_remote_copy(
                src_ref=place,
                dst_ref=place,
                send_sem=send_sem.at[k - 1],
                recv_sem=recv_sem.at[k - 1],
                device_id=sibling,
                device_id_type=MESH,
            ).wait_recv()
            to_sibling(k).start()

    keep.wait()
    sibling_block = block + 1 - 2 * core

    def from_sibling(k):
        place = kv_ref.at[sibling_block - 2 * k]
        pltpu.make_async_remote_copy(
            src_ref=place,
            dst_ref=place,
            send_sem=near_send.at[k],
            recv_sem=near_recv.at[k],
            device_id=sibling,
            device_id_type=MESH,
        ).wait_recv()

    to_sibling(0).wait_send()
    from_sibling(0)
    for k in range(1, SEEN_CHIPS + 1):

        @pl.when(chip - k >= 0)
        def _(k=k):
            to_sibling(k).wait_send()
            from_sibling(k)

        @pl.when(chip + k < chips)
        def _(k=k):
            to_chip(k).wait_send()


def turn_and_share(projected, cosine, sine, replicas):
    rows = projected.shape[0]
    vmem = pl.BlockSpec(memory_space=VMEM)
    return pl.pallas_call(
        turn_kernel,
        out_shape=(
            jax.ShapeDtypeStruct((rows, GROUP * HD), jnp.bfloat16),
            jax.ShapeDtypeStruct((replicas, rows, 2 * HD), jnp.bfloat16),
        ),
        in_specs=[vmem, vmem, vmem],
        out_specs=(vmem, pl.BlockSpec(memory_space=pltpu.HBM)),
        scratch_shapes=[
            VMEM((rows, 2 * HD), jnp.bfloat16),
            DMA,
            DMA((SEEN_CHIPS,)),
            DMA((SEEN_CHIPS,)),
            DMA((SEEN_CHIPS + 1,)),
            DMA((SEEN_CHIPS + 1,)),
        ],
        compiler_params=pltpu.CompilerParams(
            collective_id=4, has_side_effects=True, vmem_limit_bytes=24 * 2**20
        ),
        cost_estimate=pl.CostEstimate(flops=10**7, bytes_accessed=10**7, transcendentals=0),
    )(projected, cosine, sine)


def per_device(
    tokens, norm_gain, project_weight, project_bias, output_weight, source_row, segment_id
):
    local_rows = tokens.shape[0]
    replicas = lax.axis_size("dp") * lax.axis_size("ctx")
    first_row = lax.axis_index(("dp", "ctx")) * local_rows
    places = jnp.stack([source_row, segment_id])
    normed, shuffled, spots = normalise(tokens, norm_gain, output_weight, places, replicas)
    out_columns = lax.all_gather(shuffled, ("dp", "ctx"), axis=0)
    projected = project(normed, project_weight.reshape(project_weight.shape[0], -1), project_bias)
    start = spots[0]
    cosine, sine = angle_tables(lax.rem(spots[1], PACK))
    cosine = jnp.concatenate([cosine, cosine], axis=1)
    sine = jnp.concatenate([-sine, sine], axis=1)
    queries, both = turn_and_share(projected, cosine, sine, replicas)
    attended = attend(first_row, start, queries, both.reshape(-1, 2 * HD))
    return project_out(attended, out_columns)


def solution(mesh):
    placed = (
        P(("dp", "ctx"), "tensor"),
        P(),
        P(None, "tensor", None),
        P("tensor", None),
        P("tensor", None),
        P(("dp", "ctx")),
        P(("dp", "ctx")),
    )
    return jax.shard_map(
        per_device,
        mesh=mesh,
        in_specs=placed,
        out_specs=P(("dp", "ctx", "tensor"), None),
        check_vma=False,
    )
```

```python
import jax
import jax.numpy as jnp
import numpy as np
from jax import lax
from jax.experimental import pallas as pl
from jax.experimental.pallas import tpu as pltpu
from jax.sharding import PartitionSpec as P

HD = 128
GROUP = 4
PACK = 4096
DOC_IDS = 12
N_T = 8
SUBS = 4
DEPTH = 2
MESH = pl.DeviceIdType.MESH
VMEM = pltpu.VMEM
DMA = pltpu.SemaphoreType.DMA


def peer(index):
    return {"tensor": index}


def greet(others):
    barrier = pltpu.get_barrier_semaphore()
    for other in others:
        pl.semaphore_signal(barrier, inc=1, device_id=peer(other), device_id_type=MESH)


def greeted(count):
    pl.semaphore_wait(pltpu.get_barrier_semaphore(), count)


def remote(src, dst, send_sem, recv_sem, to):
    return pltpu.make_async_remote_copy(
        src_ref=src,
        dst_ref=dst,
        send_sem=send_sem,
        recv_sem=recv_sem,
        device_id=peer(to),
        device_id_type=MESH,
    )


def all_others(me):
    return [lax.rem(me + d, N_T) for d in range(1, N_T)]


class Gather:
    def __init__(self, own_ref, buf, run_of, send_sem, recv_sem):
        me = lax.axis_index("tensor")
        y = lax.rem(me, 4)
        base = me - y
        self.me = me
        self.own_ref, self.buf, self.run_of = own_ref, buf, run_of
        self.send_sem, self.recv_sem = send_sem, recv_sem
        self.up = base + lax.rem(y + 1, 4)
        self.down = base + lax.rem(y + 3, 4)
        far = base + lax.rem(y + 2, 4)

        def across(t):
            return lax.rem(t + 4, N_T)

        self.pair = across(me)
        self.owner = [
            self.down,
            self.up,
            self.pair,
            far,
            across(self.down),
            across(self.up),
            across(far),
        ]
        self.started = []

    def send(self, src, owner, kind, s, to):
        copy = remote(
            self.run_of(src, s),
            self.run_of(self.buf.at[owner], s),
            self.send_sem.at[len(self.started)],
            self.recv_sem.at[kind, s],
            to,
        )
        copy.start()
        self.started.append(copy)

    def forward(self, which, kind, s, to):
        self.send(self.buf.at[self.owner[which]], self.owner[which], kind, s, to)

    def wait(self, kind, s):
        place = self.run_of(self.buf.at[self.owner[kind]], s)
        remote(place, place, self.send_sem.at[0], self.recv_sem.at[kind, s], self.pair).wait_recv()

    def send_own(self, s):
        self.send(self.own_ref, self.me, 2, s, self.pair)
        self.send(self.own_ref, self.me, 0, s, self.up)
        self.send(self.own_ref, self.me, 1, s, self.down)

    def run(self, use, done, between):
        for s in range(SUBS):
            self.wait(0, s)
            if s % 2 == 0:
                self.forward(0, 3, s, self.up)
            self.wait(1, s)
            if s % 2 == 1:
                self.forward(1, 3, s, self.down)
            self.wait(2, s)
            self.forward(2, 4, s, self.up)
            self.forward(2, 5, s, self.down)
            if s + DEPTH < SUBS:
                self.send_own(s + DEPTH)
            for kind in (-1, 0, 1, 2):
                use(kind, s)
            if s > 0:
                for kind in (4, 5):
                    self.wait(kind, s - 1)
                    use(kind, s - 1)
            self.wait(3, s)
            self.forward(3, 6, s, self.pair)
            use(3, s)
            between(s)
            if s > 0:
                self.last(s - 1, use, done)
        for kind in (4, 5):
            self.wait(kind, SUBS - 1)
            use(kind, SUBS - 1)
        self.last(SUBS - 1, use, done)

    def last(self, s, use, done):
        self.wait(6, s)
        use(6, s)
        done(s)

    def end(self):
        for copy in self.started:
            copy.wait_send()


GATHER_SEMS = [DMA((7 * SUBS,)), DMA((7, SUBS))]
SEEN_CHIPS = 4


def put(src, dst, send_sem, recv_sem, to):
    return pltpu.make_async_remote_copy(
        src_ref=src,
        dst_ref=dst,
        send_sem=send_sem,
        recv_sem=recv_sem,
        device_id=to,
        device_id_type=MESH,
    )


def ring_of(replica):
    per = lax.axis_size("ctx")
    return {"dp": lax.div(replica, per), "ctx": lax.rem(replica, per)}


class Columns:
    def __init__(self, w_ref, all_ref, a2a_send, a2a_recv, send_sem, recv_sem, own_sem):
        self.all_ref = all_ref
        self.a2a_send, self.a2a_recv = a2a_send, a2a_recv
        self.send_sem, self.recv_sem = send_sem, recv_sem
        self.own_sem = own_sem
        self.w_ref = w_ref
        self.me = lax.axis_index("tensor")
        per = lax.axis_size("ctx")
        dp, ctx = lax.axis_index("dp"), lax.axis_index("ctx")
        core = lax.rem(ctx, 2)
        self.replica = dp * per + ctx
        sibling = ctx + 1 - 2 * core
        up, down, far = lax.rem(ctx + 2, per), lax.rem(ctx + per - 2, per), lax.rem(ctx + 4, per)
        here, there = dp * per, (1 - dp) * per
        self.to = {
            "z": {"dp": 1 - dp},
            "up": {"ctx": up},
            "down": {"ctx": down},
            "near": {"ctx": sibling},
        }
        self.piece = {
            "own": here + ctx,
            "z": there + ctx,
            "down": here + down,
            "up": here + up,
            "z down": there + down,
            "z up": there + up,
            "far": here + far,
            "z far": there + far,
        }
        self.near_piece = {}
        for name, index in self.piece.items():
            self.near_piece[name] = index + 1 - 2 * core
        self.started = []

    def block(self, t):
        piece, columns = self.all_ref.shape[2:]
        rows = pl.ds(pl.multiple_of(self.replica * piece, piece), piece)
        return self.w_ref.at[rows, pl.ds(pl.multiple_of(t * columns, columns), columns)]

    def fetch(self):
        place = self.all_ref.at[self.replica, self.me]
        self.own = pltpu.make_async_copy(self.block(self.me), place, self.own_sem)
        self.own.start()
        self.fetches = []
        for d, other in enumerate(all_others(self.me)):
            copy = remote(self.block(other), place, self.a2a_send.at[d], self.a2a_recv.at[d], other)
            copy.start()
            self.fetches.append(copy)

    def send(self, name, way, arrives):
        place = self.all_ref.at[self.piece[name]]
        copy = put(
            place,
            place,
            self.send_sem.at[len(self.started)],
            self.recv_sem.at[arrives],
            self.to[way],
        )
        copy.start()
        self.started.append(copy)

    def wait(self, index, arrives):
        place = self.all_ref.at[index]
        put(
            place, place, self.send_sem.at[0], self.recv_sem.at[arrives], self.to["near"]
        ).wait_recv()

    ARRIVES = ("z", "down", "up", "z down", "z up", "far", "z far")

    def arrived(self, name):
        self.wait(self.piece[name], self.ARRIVES.index(name))
        self.send_near(name)

    def send_near(self, name):
        self.send(name, "near", 7 + list(self.piece).index(name))

    def step(self, s):
        if s == 0:
            self.own.wait()
            for copy in self.fetches:
                copy.wait()
            self.send("own", "z", 0)
            self.send("own", "up", 1)
            self.send("own", "down", 2)
            self.send_near("own")
        if s == 1:
            self.arrived("z")
            self.send("z", "up", 3)
            self.send("z", "down", 4)
        if s == 2:
            self.arrived("down")
            self.send("down", "up", 5)
            self.arrived("up")
        if s == 3:
            self.arrived("z up")
            self.send("z up", "down", 6)
            self.arrived("z down")
            self.arrived("far")

    def end(self):
        self.arrived("z far")
        for i, name in enumerate(self.piece):
            self.wait(self.near_piece[name], 7 + i)
        for copy in self.started:
            copy.wait_send()


class Shared:
    def __init__(self, own, kv_ref, own_sem, send_sem, recv_sem, near_send, near_recv):
        per = lax.axis_size("ctx") // 2
        ctx = lax.axis_index("ctx")
        self.per = per
        self.core = lax.rem(ctx, 2)
        self.chip = lax.axis_index("dp") * per + lax.div(ctx, 2)
        self.chips = lax.axis_size("dp") * per
        self.block = self.chip * 2 + self.core
        self.sibling = {"ctx": ctx + 1 - 2 * self.core}
        self.sibling_block = self.block + 1 - 2 * self.core
        self.own, self.kv_ref, self.own_sem = own, kv_ref, own_sem
        self.send_sem, self.recv_sem = send_sem, recv_sem
        self.near_send, self.near_recv = near_send, near_recv
        step = own.shape[0] // SUBS
        self.first = [0, (SUBS - 1) * step]
        self.rows = [(SUBS - 1) * step, step]

    def run(self, ref, s):
        return ref.at[pl.ds(self.first[s], self.rows[s])]

    def to_chip(self, k, s):
        other = self.chip + k
        return put(
            self.run(self.own, s),
            self.run(self.kv_ref.at[self.block], s),
            self.send_sem.at[k - 1, s],
            self.recv_sem.at[k - 1, s],
            {"dp": lax.div(other, self.per), "ctx": lax.rem(other, self.per) * 2 + self.core},
        )

    def to_sibling(self, k, s):
        place = self.run(self.kv_ref.at[self.block - 2 * k], s)
        return put(
            self.run(self.own, s) if k == 0 else place,
            place,
            self.near_send.at[k, s],
            self.near_recv.at[k, s],
            self.sibling,
        )

    def keep(self, s):
        return pltpu.make_async_copy(
            self.run(self.own, s), self.run(self.kv_ref.at[self.block], s), self.own_sem.at[s]
        )

    def send(self, s):
        for k in (2, 1, 3, 4):

            @pl.when(self.chip + k < self.chips)
            def _(k=k):
                self.to_chip(k, s).start()

        self.to_sibling(0, s).start()
        self.keep(s).start()

    def pass_on(self, s):
        for k in (1, 3, 4, 2):

            @pl.when(self.chip - k >= 0)
            def _(k=k):
                place = self.run(self.kv_ref.at[self.block - 2 * k], s)
                put(
                    place,
                    place,
                    self.send_sem.at[k - 1, s],
                    self.recv_sem.at[k - 1, s],
                    self.sibling,
                ).wait_recv()
                self.to_sibling(k, s).start()

    def from_sibling(self, k, s):
        place = self.run(self.kv_ref.at[self.sibling_block - 2 * k], s)
        put(
            place, place, self.near_send.at[k, s], self.near_recv.at[k, s], self.sibling
        ).wait_recv()

    def end(self):
        for s in range(2):
            self.keep(s).wait()
            self.to_sibling(0, s).wait_send()
            self.from_sibling(0, s)
        for k in range(1, SEEN_CHIPS + 1):

            @pl.when(self.chip - k >= 0)
            def _(k=k):
                for s in range(2):
                    self.to_sibling(k, s).wait_send()
                    self.from_sibling(k, s)

            @pl.when(self.chip + k < self.chips)
            def _(k=k):
                for s in range(2):
                    self.to_chip(k, s).wait_send()


def project_kernel(
    tok_hbm,
    gain_hbm,
    source_hbm,
    segment_hbm,
    w_ref,
    bias_hbm,
    freq_hbm,
    wo_ref,
    q_ref,
    spots_ref,
    kv_ref,
    columns_ref,
    tok,
    gain_row,
    sources_row,
    segments_row,
    bias_row,
    freq_row,
    stats,
    docs,
    normed,
    buf,
    w_buf,
    total,
    own,
    load_sem,
    w_sem,
    stat_send,
    stat_recv,
    doc_send,
    doc_recv,
    gather_send,
    gather_recv,
    a2a_send,
    a2a_recv,
    col_send,
    col_recv,
    col_own,
    kv_own,
    kv_send,
    kv_recv,
    near_send,
    near_recv,
):
    me = lax.axis_index("tensor")
    replica = lax.axis_index("dp") * lax.axis_size("ctx") + lax.axis_index("ctx")
    replicas = docs.shape[0]
    rows, width = tok.shape
    features = width * N_T
    step = rows // SUBS
    others = all_others(me)
    alike = [ring_of(lax.rem(replica + d, replicas)) for d in range(1, replicas)]
    greet(others)
    for other in alike:
        pl.semaphore_signal(
            pltpu.get_barrier_semaphore(), inc=1, device_id=other, device_id_type=MESH
        )
    small = []
    for i, (src, dst) in enumerate(
        (
            (source_hbm, sources_row),
            (segment_hbm, segments_row),
            (gain_hbm.at[me], gain_row),
            (bias_hbm, bias_row),
            (freq_hbm, freq_row),
        )
    ):
        small.append(pltpu.make_async_copy(src, dst, load_sem.at[SUBS + i]))
        small[-1].start()
    token_loads = []
    for i in range(SUBS):
        cut = pl.ds(i * step, step)
        token_loads.append(pltpu.make_async_copy(tok_hbm.at[cut], tok.at[cut], load_sem.at[i]))
        token_loads[-1].start()
    gather = Gather(
        normed, buf, lambda ref, s: ref.at[pl.ds(s * step, step)], gather_send, gather_recv
    )
    w_loads = []
    for i, t in enumerate([me] + gather.owner):
        w_loads.append(
            pltpu.make_async_copy(
                w_ref.at[pl.ds(pl.multiple_of(t * width, width), width)], w_buf.at[i], w_sem.at[i]
            )
        )
        w_loads[-1].start()

    for copy in small:
        copy.wait()
    sources = sources_row[...]
    segments = segments_row[...]
    row = replica * rows + lax.broadcasted_iota(jnp.int32, (1, rows), 1)
    none = rows * replicas
    lane = lax.broadcasted_iota(jnp.int32, (8, 128), 1)
    line = lax.broadcasted_iota(jnp.int32, (8, 128), 0)
    table = jnp.full((8, 128), none, jnp.int32)
    for doc in range(DOC_IDS):
        of_doc = segments == doc
        first_source = jnp.min(jnp.where(of_doc, sources, none), axis=1, keepdims=True)
        first_packed = jnp.min(jnp.where(of_doc, row, none), axis=1, keepdims=True)
        found = jnp.where(line == 0, first_source, first_packed)
        table = jnp.where(lane == doc, found, table)
    docs[pl.ds(replica, 1)] = table[None]
    for i in range(SUBS):
        token_loads[i].wait()
        squares = jnp.zeros((step, 128), jnp.float32)
        for j in range(width // 128):
            part = tok[i * step : (i + 1) * step, j * 128 : (j + 1) * 128].astype(jnp.float32)
            squares = squares + part * part
        summed = jnp.sum(squares.T, axis=0, keepdims=True)
        stats[pl.ds(me, 1), :, i * step : (i + 1) * step] = jnp.broadcast_to(
            summed[None], (1, 8, step)
        )
    greeted(N_T - 1 + replicas - 1)

    stat_copies = []
    for d, other in enumerate(others):
        stat_copies.append(
            remote(stats.at[me], stats.at[me], stat_send.at[d], stat_recv.at[d], other)
        )
        stat_copies[-1].start()
    doc_copies = []
    for d, other in enumerate(alike):
        place = docs.at[replica]
        doc_copies.append(put(place, place, doc_send.at[d], doc_recv.at[d], other))
        doc_copies[-1].start()
    columns = Columns(wo_ref, columns_ref, a2a_send, a2a_recv, col_send, col_recv, col_own)
    columns.fetch()
    for copy in stat_copies:
        copy.wait()
    summed = stats[0]
    for t in range(1, N_T):
        summed = summed + stats[t]
    scale = lax.rsqrt(summed[0:1] * (1.0 / features) + 1e-06)
    for i in range(SUBS):
        along = jnp.broadcast_to(scale[:, i * step : (i + 1) * step], (128, step)).T
        for j in range(width // 128):
            cut = (slice(i * step, (i + 1) * step), slice(j * 128, (j + 1) * 128))
            gain = gain_row[:, j * 128 : (j + 1) * 128]
            normed[cut] = (tok[cut].astype(jnp.float32) * along * gain).astype(jnp.bfloat16)

    shared = Shared(own, kv_ref, kv_own, kv_send, kv_recv, near_send, near_recv)
    spots = {}

    def find_spots():
        for copy in doc_copies:
            copy.wait()
        table = docs[0]
        for r in range(1, replicas):
            table = jnp.minimum(table, docs[r])
        start = jnp.full((1, rows), -1, jnp.int32)
        place = row
        for doc in range(DOC_IDS):
            first_source = table[0:1, doc : doc + 1]
            first_packed = table[1:2, doc : doc + 1]
            later = (first_source <= row) & (first_source > start)
            start = jnp.where(later, first_source, start)
            place = jnp.where(later, row + (first_packed - first_source), place)
        spots_ref[...] = jnp.where(
            lax.broadcasted_iota(jnp.int32, (8, rows), 0) == 0, start, place
        )
        spots["position"] = lax.rem(place, PACK).astype(jnp.float32)

    def use(kind, s):
        i = kind + 1
        if s == 0:
            w_loads[i].wait()
        chunk = normed if kind < 0 else buf.at[gather.owner[kind]]
        here = slice(s * step, (s + 1) * step)
        term = jnp.dot(chunk[here, :], w_buf[i], preferred_element_type=jnp.float32)
        if kind < 0:
            total[here, :] = term
        else:
            total[here, :] += term

    def done(s):
        here = slice(s * step, (s + 1) * step)
        bias = bias_row[...].astype(jnp.float32)
        angle = (
            jnp.broadcast_to(spots["position"][:, here], (128, step)).T * freq_row[...]
        )
        cosine = jnp.cos(angle)
        sine = jnp.sin(angle)
        first = lax.broadcasted_iota(jnp.int32, (step, HD), 1) < HD // 2
        sine = jnp.where(first, -sine, sine)

        def slot(index):
            cut = slice(index * HD, (index + 1) * HD)
            return (total[here, cut] + bias[:, cut]).astype(jnp.bfloat16)

        def turned(index):
            wide = slot(index).astype(jnp.float32)
            return (wide * cosine + pltpu.roll(wide, HD // 2, 1) * sine).astype(jnp.bfloat16)

        own[here, :HD] = turned(GROUP)
        own[here, HD:] = slot(GROUP + 1)
        if s >= SUBS - 2:
            shared.send(s - SUBS + 2)
        for head in range(GROUP):
            q_ref[here, head * HD : (head + 1) * HD] = turned(head)

    for s in range(DEPTH):
        gather.send_own(s)
    find_spots()
    gather.run(use, done, columns.step)
    shared.pass_on(0)
    columns.end()
    shared.pass_on(1)
    shared.end()
    gather.end()


def project(tokens, gain, sources, segments, weight, bias, out_weight, replicas):
    rows, width = tokens.shape
    columns = weight.shape[1]
    depth, out_width = out_weight.shape
    half = HD // 2
    freqs = (1e6 ** (-(np.arange(half) * 2.0) / HD)).astype(np.float32)
    freqs = jnp.asarray(np.concatenate([freqs, freqs])[None])
    hbm = pl.BlockSpec(memory_space=pltpu.HBM)
    vmem = pl.BlockSpec(memory_space=VMEM)
    return pl.pallas_call(
        project_kernel,
        out_shape=(
            jax.ShapeDtypeStruct((rows, GROUP * HD), jnp.bfloat16),
            jax.ShapeDtypeStruct((8, rows), jnp.int32),
            jax.ShapeDtypeStruct((replicas, rows, 2 * HD), jnp.bfloat16),
            jax.ShapeDtypeStruct((replicas, N_T, depth // replicas, out_width // N_T), jnp.bfloat16),
        ),
        in_specs=[hbm] * 8,
        out_specs=(vmem, vmem, hbm, hbm),
        scratch_shapes=[
            VMEM((rows, width), jnp.bfloat16),
            VMEM((1, width), jnp.float32),
            VMEM((1, rows), jnp.int32),
            VMEM((1, rows), jnp.int32),
            VMEM((1, columns), jnp.bfloat16),
            VMEM((1, HD), jnp.float32),
            VMEM((N_T, 8, rows), jnp.float32),
            VMEM((replicas, 8, 128), jnp.int32),
            VMEM((rows, width), jnp.bfloat16),
            VMEM((N_T, rows, width), jnp.bfloat16),
            VMEM((N_T, width, columns), jnp.bfloat16),
            VMEM((rows, columns), jnp.float32),
            VMEM((rows, 2 * HD), jnp.bfloat16),
            DMA((SUBS + 5,)),
            DMA((N_T,)),
            DMA((N_T - 1,)),
            DMA((N_T - 1,)),
            DMA((replicas - 1,)),
            DMA((replicas - 1,)),
            *GATHER_SEMS,
            DMA((N_T - 1,)),
            DMA((N_T - 1,)),
            DMA((15,)),
            DMA((15,)),
            DMA,
            DMA((2,)),
            DMA((SEEN_CHIPS, 2)),
            DMA((SEEN_CHIPS, 2)),
            DMA((SEEN_CHIPS + 1, 2)),
            DMA((SEEN_CHIPS + 1, 2)),
        ],
        compiler_params=pltpu.CompilerParams(
            collective_id=1, has_side_effects=True, vmem_limit_bytes=58 * 2**20
        ),
        cost_estimate=pl.CostEstimate(
            flops=2 * rows * width * N_T * columns, bytes_accessed=10**8, transcendentals=10**5
        ),
    )(
        tokens,
        gain.reshape(N_T, 1, width),
        sources.reshape(1, rows),
        segments.reshape(1, rows),
        weight,
        bias,
        freqs,
        out_weight,
    )


def output_kernel(
    own_ref,
    w_ref,
    out_ref,
    buf,
    w_buf,
    total,
    ready,
    gather_send,
    gather_recv,
    w_sem,
    out_send,
    out_recv,
    own_sem,
):
    me = lax.axis_index("tensor")
    part = own_ref.shape[1] // SUBS
    others = all_others(me)
    greet(others)

    def run_of(ref, s):
        return ref.at[:, pl.ds(s * part, part)]

    gather = Gather(own_ref, buf, run_of, gather_send, gather_recv)
    loads = []
    for i, t in enumerate([me] + gather.owner):
        loads.append(pltpu.make_async_copy(w_ref.at[:, t], w_buf.at[i], w_sem.at[i]))
        loads[-1].start()
    greeted(N_T - 1)
    depth = own_ref.shape[2]
    columns = total.shape[1]
    place = pl.ds(pl.multiple_of(me * columns, columns), columns)
    copies = []

    def use(kind, s):
        i = kind + 1
        if s == 0:
            loads[i].wait()
        chunk = own_ref if kind < 0 else buf.at[gather.owner[kind]]
        weight = w_buf[i].reshape(depth, columns)
        rows = chunk[:, s * part : (s + 1) * part, :].reshape(N_T * part, depth)
        term = jnp.dot(rows, weight, preferred_element_type=jnp.float32)
        term = term.astype(jnp.bfloat16).astype(jnp.float32)
        here = slice(s * N_T * part, (s + 1) * N_T * part)
        if kind < 0:
            total[here, :] = term
        else:
            total[here, :] += term

    def done(s):
        here = slice(s * N_T * part, (s + 1) * N_T * part)
        ready[s] = total[here, :].astype(jnp.bfloat16).reshape(N_T, part, columns)
        target = out_ref.at[pl.ds(s * part, part), place]
        for d, other in enumerate(others):
            copies.append(
                remote(ready.at[s, other], target, out_send.at[d, s], out_recv.at[d, s], other)
            )
            copies[-1].start()
        copies.append(pltpu.make_async_copy(ready.at[s, me], target, own_sem.at[s]))
        copies[-1].start()

    for s in range(DEPTH):
        gather.send_own(s)
    gather.run(use, done, lambda s: None)
    for copy in copies:
        copy.wait()
    gather.end()


def project_out(attended, weight):
    rows, depth = attended.shape
    columns = weight.shape[3]
    each = rows // N_T
    return pl.pallas_call(
        output_kernel,
        out_shape=jax.ShapeDtypeStruct((each, columns * N_T), jnp.bfloat16),
        in_specs=[pl.BlockSpec(memory_space=VMEM), pl.BlockSpec(memory_space=pltpu.HBM)],
        out_specs=pl.BlockSpec(memory_space=pltpu.HBM),
        scratch_shapes=[
            VMEM((N_T, N_T, each, depth), jnp.bfloat16),
            VMEM((N_T, weight.shape[0], weight.shape[2], columns), jnp.bfloat16),
            VMEM((rows, columns), jnp.float32),
            VMEM((SUBS, N_T, each // SUBS, columns), jnp.bfloat16),
            *GATHER_SEMS,
            DMA((N_T,)),
            DMA((N_T - 1, SUBS)),
            DMA((N_T - 1, SUBS)),
            DMA((SUBS,)),
        ],
        compiler_params=pltpu.CompilerParams(
            collective_id=3, has_side_effects=True, vmem_limit_bytes=48 * 2**20
        ),
        cost_estimate=pl.CostEstimate(
            flops=2 * rows * depth * N_T * columns, bytes_accessed=10**8, transcendentals=0
        ),
    )(attended.reshape(N_T, each, depth), weight)


TILE_Q = 256
SEEN_BLOCKS = 2 * SEEN_CHIPS
TILE_K = 256
LOW = -1e30


def attend_kernel(
    spots_hbm, q_hbm, kv_hbm, out_ref, starts, spots_ref, q_ref, kv_ref, load_sem, kv_sem
):
    rows = q_ref.shape[0]
    block = lax.axis_index("dp") * lax.axis_size("ctx") + lax.axis_index("ctx")
    first_row = block * rows
    loads = [
        pltpu.make_async_copy(spots_hbm, starts, load_sem.at[0]),
        pltpu.make_async_copy(spots_hbm, spots_ref, load_sem.at[1]),
        pltpu.make_async_copy(q_hbm, q_ref, load_sem.at[2]),
    ]
    for load in loads:
        load.start()

    def kv_load(back):
        return pltpu.make_async_copy(
            kv_hbm.at[block - back],
            kv_ref.at[pl.ds(pl.multiple_of((block - back) * rows, rows), rows)],
            kv_sem.at[back],
        )

    for back in range(SEEN_BLOCKS + 1):

        @pl.when(block - back >= 0)
        def _(back=back):
            kv_load(back).start()

    for load in loads:
        load.wait()
    for back in range(SEEN_BLOCKS + 1):

        @pl.when(block - back >= 0)
        def _(back=back):
            kv_load(back).wait()

    heads = q_ref.shape[1] // HD
    factor = HD**-0.5 * 1.4426950408889634
    for a in range(rows // TILE_Q):
        base = first_row + a * TILE_Q
        start = spots_ref[0:1, a * TILE_Q : (a + 1) * TILE_Q]
        query_row = base + lax.broadcasted_iota(jnp.int32, (1, TILE_Q), 1)
        low_tile = lax.div(starts[0, a * TILE_Q], TILE_K)
        high_tile = lax.div(base + TILE_Q, TILE_K)

        def one(i, carry, a=a, start=start, query_row=query_row, high_tile=high_tile):
            tile = high_tile - 1 - i
            cut = pl.ds(pl.multiple_of(tile * TILE_K, TILE_K), TILE_K)
            keys = kv_ref[cut, :HD]
            values = kv_ref[cut, HD:].T
            key_row = tile * TILE_K + lax.broadcasted_iota(jnp.int32, (TILE_K, TILE_Q), 0)
            allowed = (key_row >= start) & (key_row <= query_row)
            after = []
            for h in range(heads):
                top, denominator, weighted = carry[h]
                query = q_ref[a * TILE_Q : (a + 1) * TILE_Q, h * HD : (h + 1) * HD]
                scores = lax.dot_general(
                    keys, query, (((1,), (1,)), ((), ())), preferred_element_type=jnp.float32
                )
                scores = jnp.where(allowed, scores * factor, 2 * LOW)
                new_top = jnp.maximum(top, jnp.max(scores, axis=0, keepdims=True))
                weights = jnp.exp2(scores - new_top)
                shrink = jnp.exp2(top - new_top)
                denominator = denominator * shrink + jnp.sum(weights, axis=0, keepdims=True)
                coarse = weights.astype(jnp.bfloat16)
                fine = (weights - coarse.astype(jnp.float32)).astype(jnp.bfloat16)
                weighted = weighted * shrink
                weighted += jnp.dot(values, coarse, preferred_element_type=jnp.float32)
                weighted += jnp.dot(values, fine, preferred_element_type=jnp.float32)
                after.append((new_top, denominator, weighted))
            return tuple(after)

        begin = (
            jnp.full((1, TILE_Q), LOW, jnp.float32),
            jnp.zeros((1, TILE_Q), jnp.float32),
            jnp.zeros((HD, TILE_Q), jnp.float32),
        )
        ended = lax.fori_loop(0, high_tile - low_tile, one, (begin,) * heads)
        for h in range(heads):
            _, denominator, weighted = ended[h]
            out_ref[a * TILE_Q : (a + 1) * TILE_Q, h * HD : (h + 1) * HD] = (
                (weighted / denominator).T.astype(jnp.bfloat16)
            )


def attend(spots, queries, both):
    blocks, rows, width = both.shape
    hbm = pl.BlockSpec(memory_space=pltpu.HBM)
    return pl.pallas_call(
        attend_kernel,
        out_shape=jax.ShapeDtypeStruct(queries.shape, jnp.bfloat16),
        in_specs=[hbm, hbm, hbm],
        out_specs=pl.BlockSpec(memory_space=VMEM),
        scratch_shapes=[
            pltpu.SMEM(spots.shape, jnp.int32),
            VMEM(spots.shape, jnp.int32),
            VMEM(queries.shape, jnp.bfloat16),
            VMEM((blocks * rows, width), jnp.bfloat16),
            DMA((3,)),
            DMA((SEEN_BLOCKS + 1,)),
        ],
        compiler_params=pltpu.CompilerParams(vmem_limit_bytes=58 * 2**20),
        cost_estimate=pl.CostEstimate(flops=10**9, bytes_accessed=10**7, transcendentals=10**7),
    )(spots, queries, both)


def per_device(
    tokens, norm_gain, project_weight, project_bias, output_weight, source_row, segment_id
):
    replicas = lax.axis_size("dp") * lax.axis_size("ctx")
    flat_weight = project_weight.reshape(project_weight.shape[0], -1)
    queries, spots, both, out_columns = project(
        tokens, norm_gain, source_row, segment_id, flat_weight, project_bias, output_weight, replicas
    )
    attended = attend(spots, queries, both)
    return project_out(attended, out_columns)


def solution(mesh):
    placed = (
        P(("dp", "ctx"), "tensor"),
        P(),
        P(None, "tensor", None),
        P("tensor", None),
        P("tensor", None),
        P(("dp", "ctx")),
        P(("dp", "ctx")),
    )
    return jax.shard_map(
        per_device,
        mesh=mesh,
        in_specs=placed,
        out_specs=P(("dp", "ctx", "tensor"), None),
        check_vma=False,
    )
```

```python
import jax
import jax.numpy as jnp
import numpy as np
from jax import lax
from jax.experimental import pallas as pl
from jax.experimental.pallas import tpu as pltpu
from jax.sharding import PartitionSpec as P

HD = 128
GROUP = 4
PACK = 4096
DOC_IDS = 12
N_T = 8
SUBS = 4
DEPTH = 2
CUTS = (0, 128, 256, 384, 512)
OVER_Z = ((), ())
OUT_OVER_Z = ((1,), (2,))
BATCHES = ((0, 2), (2, 3), (3, 4))
MESH = pl.DeviceIdType.MESH
VMEM = pltpu.VMEM
DMA = pltpu.SemaphoreType.DMA


def peer(index):
    return {"tensor": index}


def greet(others):
    barrier = pltpu.get_barrier_semaphore()
    for other in others:
        pl.semaphore_signal(barrier, inc=1, device_id=peer(other), device_id_type=MESH)


def greeted(count):
    pl.semaphore_wait(pltpu.get_barrier_semaphore(), count)


def remote(src, dst, send_sem, recv_sem, to):
    return pltpu.make_async_remote_copy(
        src_ref=src,
        dst_ref=dst,
        send_sem=send_sem,
        recv_sem=recv_sem,
        device_id=peer(to),
        device_id_type=MESH,
    )


def all_others(me):
    return [lax.rem(me + d, N_T) for d in range(1, N_T)]


class Gather:
    def __init__(self, own_ref, buf, run_of, send_sem, recv_sem, over_z=((), ())):
        self.over_z = over_z
        me = lax.axis_index("tensor")
        y = lax.rem(me, 4)
        base = me - y
        self.me = me
        self.own_ref, self.buf, self.run_of = own_ref, buf, run_of
        self.send_sem, self.recv_sem = send_sem, recv_sem
        self.up = base + lax.rem(y + 1, 4)
        self.down = base + lax.rem(y + 3, 4)
        far = base + lax.rem(y + 2, 4)

        def across(t):
            return lax.rem(t + 4, N_T)

        self.pair = across(me)
        self.owner = [
            self.down,
            self.up,
            self.pair,
            far,
            across(self.down),
            across(self.up),
            across(far),
        ]
        self.started = []

    def send(self, src, owner, kind, s, to):
        copy = remote(
            self.run_of(src, s),
            self.run_of(self.buf.at[owner], s),
            self.send_sem.at[len(self.started)],
            self.recv_sem.at[kind, s],
            to,
        )
        copy.start()
        self.started.append(copy)

    def forward(self, which, kind, s, to):
        self.send(self.buf.at[self.owner[which]], self.owner[which], kind, s, to)

    def wait(self, kind, s):
        place = self.run_of(self.buf.at[self.owner[kind]], s)
        remote(place, place, self.send_sem.at[0], self.recv_sem.at[kind, s], self.pair).wait_recv()

    def send_own(self, s):
        self.send(self.own_ref, self.me, 2, s, self.pair)
        self.send(self.own_ref, self.me, 0, s, self.up)
        self.send(self.own_ref, self.me, 1, s, self.down)

    def run(self, use, done, between):
        for s in range(SUBS):
            self.wait(0, s)
            if s % 2 == 0:
                self.forward(0, 3, s, self.up)
            if s in self.over_z[0]:
                self.forward(0, 4, s, self.pair)
            self.wait(1, s)
            if s % 2 == 1:
                self.forward(1, 3, s, self.down)
            if s in self.over_z[1]:
                self.forward(1, 5, s, self.pair)
            self.wait(2, s)
            if s not in self.over_z[0]:
                self.forward(2, 4, s, self.up)
            if s not in self.over_z[1]:
                self.forward(2, 5, s, self.down)
            if s + DEPTH < SUBS:
                self.send_own(s + DEPTH)
            for kind in (-1, 0, 1, 2):
                use(kind, s)
            if s > 0:
                self.across_sides(s - 1, use)
            self.wait(3, s)
            self.forward(3, 6, s, self.pair)
            use(3, s)
            between(s)
            if s > 0:
                self.last(s - 1, use, done)
        self.across_sides(SUBS - 1, use)
        self.last(SUBS - 1, use, done)

    def across_sides(self, s, use):
        self.wait(4, s)
        use(4, s)
        self.wait(5, s)
        use(5, s)

    def last(self, s, use, done):
        self.wait(6, s)
        use(6, s)
        done(s)

    def end(self):
        for copy in self.started:
            copy.wait_send()


GATHER_SEMS = [DMA((7 * SUBS,)), DMA((7, SUBS))]
SEEN_CHIPS = 4


def put(src, dst, send_sem, recv_sem, to):
    return pltpu.make_async_remote_copy(
        src_ref=src,
        dst_ref=dst,
        send_sem=send_sem,
        recv_sem=recv_sem,
        device_id=to,
        device_id_type=MESH,
    )


def ring_of(replica):
    per = lax.axis_size("ctx")
    return {"dp": lax.div(replica, per), "ctx": lax.rem(replica, per)}


class Columns:
    def __init__(self, w_ref, all_ref, a2a_send, a2a_recv, send_sem, recv_sem, own_sem):
        self.all_ref = all_ref
        self.a2a_send, self.a2a_recv = a2a_send, a2a_recv
        self.send_sem, self.recv_sem = send_sem, recv_sem
        self.own_sem = own_sem
        self.w_ref = w_ref
        self.me = lax.axis_index("tensor")
        per = lax.axis_size("ctx")
        dp, ctx = lax.axis_index("dp"), lax.axis_index("ctx")
        core = lax.rem(ctx, 2)
        self.replica = dp * per + ctx
        sibling = ctx + 1 - 2 * core
        up, down, far = lax.rem(ctx + 2, per), lax.rem(ctx + per - 2, per), lax.rem(ctx + 4, per)
        here, there = dp * per, (1 - dp) * per
        self.to = {
            "z": {"dp": 1 - dp},
            "up": {"ctx": up},
            "down": {"ctx": down},
            "near": {"ctx": sibling},
        }
        self.piece = {
            "own": here + ctx,
            "z": there + ctx,
            "down": here + down,
            "up": here + up,
            "z down": there + down,
            "z up": there + up,
            "far": here + far,
            "z far": there + far,
        }
        self.near_piece = {}
        for name, index in self.piece.items():
            self.near_piece[name] = index + 1 - 2 * core
        self.started = []

    def block(self, t):
        piece, columns = self.all_ref.shape[2:]
        rows = pl.ds(pl.multiple_of(self.replica * piece, piece), piece)
        return self.w_ref.at[rows, pl.ds(pl.multiple_of(t * columns, columns), columns)]

    def fetch(self):
        place = self.all_ref.at[self.replica, self.me]
        self.own = pltpu.make_async_copy(self.block(self.me), place, self.own_sem)
        self.own.start()
        self.fetches = []
        for d, other in enumerate(all_others(self.me)):
            copy = remote(self.block(other), place, self.a2a_send.at[d], self.a2a_recv.at[d], other)
            copy.start()
            self.fetches.append(copy)

    def send(self, name, way, arrives):
        place = self.all_ref.at[self.piece[name]]
        copy = put(
            place,
            place,
            self.send_sem.at[len(self.started)],
            self.recv_sem.at[arrives],
            self.to[way],
        )
        copy.start()
        self.started.append(copy)

    def wait(self, index, arrives):
        place = self.all_ref.at[index]
        put(
            place, place, self.send_sem.at[0], self.recv_sem.at[arrives], self.to["near"]
        ).wait_recv()

    ARRIVES = ("z", "down", "up", "z down", "z up", "far", "z far")

    def arrived(self, name):
        self.wait(self.piece[name], self.ARRIVES.index(name))
        self.send_near(name)

    def send_near(self, name):
        self.send(name, "near", 7 + list(self.piece).index(name))

    def step(self, s):
        if s == 0:
            self.own.wait()
            for copy in self.fetches:
                copy.wait()
            self.send("own", "z", 0)
            self.send("own", "up", 1)
            self.send("own", "down", 2)
            self.send_near("own")
        if s == 1:
            self.arrived("z")
            self.send("z", "up", 3)
            self.send("z", "down", 4)
        if s == 2:
            self.arrived("down")
            self.send("down", "up", 5)
            self.arrived("up")
        if s == 3:
            self.arrived("z up")
            self.send("z up", "down", 6)
            self.arrived("z down")
            self.arrived("far")

    def end(self):
        self.arrived("z far")
        for i, name in enumerate(self.piece):
            self.wait(self.near_piece[name], 7 + i)
        for copy in self.started:
            copy.wait_send()


class Shared:
    def __init__(self, own, kv_ref, own_sem, send_sem, recv_sem, near_send, near_recv, along_send):
        per = lax.axis_size("ctx") // 2
        ctx = lax.axis_index("ctx")
        self.per = per
        self.core = lax.rem(ctx, 2)
        self.chip = lax.axis_index("dp") * per + lax.div(ctx, 2)
        self.chips = lax.axis_size("dp") * per
        self.block = self.chip * 2 + self.core
        self.sibling = {"ctx": ctx + 1 - 2 * self.core}
        self.sibling_block = self.block + 1 - 2 * self.core
        self.own, self.kv_ref, self.own_sem = own, kv_ref, own_sem
        self.send_sem, self.recv_sem = send_sem, recv_sem
        self.near_send, self.near_recv = near_send, near_recv
        self.along_send = along_send
        self.x = lax.rem(self.chip, per)

    def run(self, ref, s):
        first, last = (CUTS[cut] for cut in BATCHES[s])
        return ref.at[pl.ds(first, last - first)]

    def to_chip(self, k, s):
        other = self.chip + k
        return put(
            self.run(self.own, s),
            self.run(self.kv_ref.at[self.block], s),
            self.send_sem.at[k - 1, s],
            self.recv_sem.at[k - 1, s],
            {"dp": lax.div(other, self.per), "ctx": lax.rem(other, self.per) * 2 + self.core},
        )

    def to_sibling(self, k, s):
        place = self.run(self.kv_ref.at[self.block - 2 * k], s)
        return put(
            self.run(self.own, s) if k == 0 else place,
            place,
            self.near_send.at[k, s],
            self.near_recv.at[k, s],
            self.sibling,
        )

    def keep(self, s):
        return pltpu.make_async_copy(
            self.run(self.own, s), self.run(self.kv_ref.at[self.block], s), self.own_sem.at[s]
        )

    def sends(self, act):
        for k in (2, 1, 3):

            @pl.when(self.x + k < self.per)
            def _(k=k):
                act(k)

        @pl.when(self.chip + self.per < self.chips)
        def _():
            act(self.per)

    def send(self, s):
        self.sends(lambda k: self.to_chip(k, s).start())
        self.to_sibling(0, s).start()
        self.keep(s).start()

    def along(self, m, s):
        place = self.run(self.kv_ref.at[self.block - 2 * self.per], s)
        return put(
            place,
            place,
            self.along_send.at[m - 1, s],
            self.recv_sem.at[self.per - m - 1, s],
            {"ctx": (self.x - m) * 2 + self.core},
        )

    def relays(self, act):
        for m in (2, 1, 3):

            @pl.when((self.chip >= self.per) & (self.x >= m))
            def _(m=m):
                act(m)

    def pass_on(self, s):
        for k in (4, 1, 3, 2):

            @pl.when(self.chip - k >= 0)
            def _(k=k):
                place = self.run(self.kv_ref.at[self.block - 2 * k], s)
                put(
                    place,
                    place,
                    self.send_sem.at[k - 1, s],
                    self.recv_sem.at[k - 1, s],
                    self.sibling,
                ).wait_recv()

            if k == self.per:
                self.relays(lambda m: self.along(m, s).start())

            @pl.when(self.chip - k >= 0)
            def _(k=k):
                self.to_sibling(k, s).start()

    def from_sibling(self, k, s):
        place = self.run(self.kv_ref.at[self.sibling_block - 2 * k], s)
        put(
            place, place, self.near_send.at[k, s], self.near_recv.at[k, s], self.sibling
        ).wait_recv()

    def end(self):
        for s in range(len(BATCHES)):
            self.keep(s).wait()
            self.to_sibling(0, s).wait_send()
            self.from_sibling(0, s)
        for k in range(1, SEEN_CHIPS + 1):

            @pl.when(self.chip - k >= 0)
            def _(k=k):
                for s in range(len(BATCHES)):
                    self.to_sibling(k, s).wait_send()
                    self.from_sibling(k, s)

        for s in range(len(BATCHES)):
            self.sends(lambda k, s=s: self.to_chip(k, s).wait_send())
            self.relays(lambda m, s=s: self.along(m, s).wait_send())


def project_kernel(
    tok_hbm,
    gain_hbm,
    source_hbm,
    segment_hbm,
    w_ref,
    bias_hbm,
    freq_hbm,
    wo_ref,
    q_ref,
    spots_ref,
    kv_ref,
    columns_ref,
    tok,
    gain_rows,
    sources_row,
    segments_row,
    bias_row,
    freq_row,
    stats,
    docs,
    scales,
    cosines,
    sines,
    normed,
    buf,
    w_buf,
    total,
    own,
    load_sem,
    w_sem,
    stat_send,
    stat_recv,
    doc_send,
    doc_recv,
    gather_send,
    gather_recv,
    a2a_send,
    a2a_recv,
    col_send,
    col_recv,
    col_own,
    kv_own,
    kv_send,
    kv_recv,
    near_send,
    near_recv,
    along_send,
):
    me = lax.axis_index("tensor")
    replica = lax.axis_index("dp") * lax.axis_size("ctx") + lax.axis_index("ctx")
    replicas = docs.shape[0]
    rows, width = tok.shape
    features = width * N_T
    step = rows // SUBS
    others = all_others(me)
    alike = [ring_of(lax.rem(replica + d, replicas)) for d in range(1, replicas)]
    greet(others)
    for other in alike:
        pl.semaphore_signal(
            pltpu.get_barrier_semaphore(), inc=1, device_id=other, device_id_type=MESH
        )
    small = []
    for i, (src, dst) in enumerate(
        (
            (source_hbm, sources_row),
            (segment_hbm, segments_row),
            (gain_hbm, gain_rows),
            (bias_hbm, bias_row),
            (freq_hbm, freq_row),
        )
    ):
        small.append(pltpu.make_async_copy(src, dst, load_sem.at[SUBS + i]))
        small[-1].start()
    token_loads = []
    for i in range(SUBS):
        cut = pl.ds(i * step, step)
        token_loads.append(pltpu.make_async_copy(tok_hbm.at[cut], tok.at[cut], load_sem.at[i]))
        token_loads[-1].start()

    def run_of(ref, s):
        return ref.at[pl.ds(CUTS[s], CUTS[s + 1] - CUTS[s])]

    gather = Gather(tok, buf, run_of, gather_send, gather_recv, OVER_Z)
    w_loads = []
    for i, t in enumerate([me] + gather.owner):
        w_loads.append(
            pltpu.make_async_copy(
                w_ref.at[pl.ds(pl.multiple_of(t * width, width), width)], w_buf.at[i], w_sem.at[i]
            )
        )
        w_loads[-1].start()

    for copy in small:
        copy.wait()
    sources = sources_row[...]
    segments = segments_row[...]
    row = replica * rows + lax.broadcasted_iota(jnp.int32, (1, rows), 1)
    none = rows * replicas
    lane = lax.broadcasted_iota(jnp.int32, (8, 128), 1)
    line = lax.broadcasted_iota(jnp.int32, (8, 128), 0)
    table = jnp.full((8, 128), none, jnp.int32)
    for doc in range(DOC_IDS):
        of_doc = segments == doc
        first_source = jnp.min(jnp.where(of_doc, sources, none), axis=1, keepdims=True)
        first_packed = jnp.min(jnp.where(of_doc, row, none), axis=1, keepdims=True)
        found = jnp.where(line == 0, first_source, first_packed)
        table = jnp.where(lane == doc, found, table)
    docs[pl.ds(replica, 1)] = table[None]
    for i in range(SUBS):
        token_loads[i].wait()
        squares = jnp.zeros((step, 128), jnp.float32)
        for j in range(width // 128):
            part = tok[i * step : (i + 1) * step, j * 128 : (j + 1) * 128].astype(jnp.float32)
            squares = squares + part * part
        summed = jnp.sum(squares.T, axis=0, keepdims=True)
        stats[pl.ds(me, 1), :, i * step : (i + 1) * step] = jnp.broadcast_to(
            summed[None], (1, 8, step)
        )
    greeted(N_T - 1 + replicas - 1)

    stat_copies = []
    for d, other in enumerate(others):
        stat_copies.append(
            remote(stats.at[me], stats.at[me], stat_send.at[d], stat_recv.at[d], other)
        )
        stat_copies[-1].start()
    doc_copies = []
    for d, other in enumerate(alike):
        place = docs.at[replica]
        doc_copies.append(put(place, place, doc_send.at[d], doc_recv.at[d], other))
        doc_copies[-1].start()
    for s in range(DEPTH):
        gather.send_own(s)
    columns = Columns(wo_ref, columns_ref, a2a_send, a2a_recv, col_send, col_recv, col_own)
    columns.fetch()
    for copy in stat_copies:
        copy.wait()
    summed = stats[0]
    for t in range(1, N_T):
        summed = summed + stats[t]
    scale = lax.rsqrt(summed[0:1] * (1.0 / features) + 1e-06)
    for i in range(SUBS):
        here = slice(i * step, (i + 1) * step)
        scales[here, :] = jnp.broadcast_to(scale[:, here], (128, step)).T

    shared = Shared(own, kv_ref, kv_own, kv_send, kv_recv, near_send, near_recv, along_send)
    def find_spots():
        for copy in doc_copies:
            copy.wait()
        table = docs[0]
        for r in range(1, replicas):
            table = jnp.minimum(table, docs[r])
        start = jnp.full((1, rows), -1, jnp.int32)
        place = row
        for doc in range(DOC_IDS):
            first_source = table[0:1, doc : doc + 1]
            first_packed = table[1:2, doc : doc + 1]
            later = (first_source <= row) & (first_source > start)
            start = jnp.where(later, first_source, start)
            place = jnp.where(later, row + (first_packed - first_source), place)
        spots_ref[...] = jnp.where(
            lax.broadcasted_iota(jnp.int32, (8, rows), 0) == 0, start, place
        )
        position = lax.rem(place, PACK).astype(jnp.float32)
        first = lax.broadcasted_iota(jnp.int32, (step, HD), 1) < HD // 2
        for i in range(SUBS):
            here = slice(i * step, (i + 1) * step)
            angle = jnp.broadcast_to(position[:, here], (128, step)).T * freq_row[...]
            cosines[here, :] = jnp.cos(angle)
            sine = jnp.sin(angle)
            sines[here, :] = jnp.where(first, -sine, sine)

    def use(kind, s):
        i = kind + 1
        if s == 0:
            w_loads[i].wait()
        owner = me if kind < 0 else gather.owner[kind]
        chunk = tok if kind < 0 else buf.at[owner]
        here = slice(CUTS[s], CUTS[s + 1])
        along = scales[here, :]
        for j in range(width // 128):
            cut = slice(j * 128, (j + 1) * 128)
            wide = chunk[here, cut].astype(jnp.float32)
            normed[here, cut] = (wide * along * gain_rows[owner, :, cut]).astype(jnp.bfloat16)
        term = jnp.dot(normed[here, :], w_buf[i], preferred_element_type=jnp.float32)
        if kind < 0:
            total[here, :] = term
        else:
            total[here, :] += term

    def done(s):
        here = slice(CUTS[s], CUTS[s + 1])
        bias = bias_row[...].astype(jnp.float32)
        cosine = cosines[here, :]
        sine = sines[here, :]

        def slot(index):
            cut = slice(index * HD, (index + 1) * HD)
            return (total[here, cut] + bias[:, cut]).astype(jnp.bfloat16)

        def turned(index):
            wide = slot(index).astype(jnp.float32)
            return (wide * cosine + pltpu.roll(wide, HD // 2, 1) * sine).astype(jnp.bfloat16)

        own[here, :HD] = turned(GROUP)
        own[here, HD:] = slot(GROUP + 1)
        for batch, (_, end) in enumerate(BATCHES):
            if end == s + 1:
                shared.send(batch)
        for head in range(GROUP):
            q_ref[here, head * HD : (head + 1) * HD] = turned(head)

    find_spots()
    gather.run(use, done, columns.step)
    shared.pass_on(0)
    shared.pass_on(1)
    columns.end()
    shared.pass_on(2)
    shared.end()
    gather.end()


def project(tokens, gain, sources, segments, weight, bias, out_weight, replicas):
    rows, width = tokens.shape
    columns = weight.shape[1]
    depth, out_width = out_weight.shape
    half = HD // 2
    freqs = (1e6 ** (-(np.arange(half) * 2.0) / HD)).astype(np.float32)
    freqs = jnp.asarray(np.concatenate([freqs, freqs])[None])
    hbm = pl.BlockSpec(memory_space=pltpu.HBM)
    vmem = pl.BlockSpec(memory_space=VMEM)
    return pl.pallas_call(
        project_kernel,
        out_shape=(
            jax.ShapeDtypeStruct((rows, GROUP * HD), jnp.bfloat16),
            jax.ShapeDtypeStruct((8, rows), jnp.int32),
            jax.ShapeDtypeStruct((replicas, rows, 2 * HD), jnp.bfloat16),
            jax.ShapeDtypeStruct((replicas, N_T, depth // replicas, out_width // N_T), jnp.bfloat16),
        ),
        in_specs=[hbm] * 8,
        out_specs=(vmem, vmem, hbm, hbm),
        scratch_shapes=[
            VMEM((rows, width), jnp.bfloat16),
            VMEM((N_T, 1, width), jnp.float32),
            VMEM((1, rows), jnp.int32),
            VMEM((1, rows), jnp.int32),
            VMEM((1, columns), jnp.bfloat16),
            VMEM((1, HD), jnp.float32),
            VMEM((N_T, 8, rows), jnp.float32),
            VMEM((replicas, 8, 128), jnp.int32),
            VMEM((rows, HD), jnp.float32),
            VMEM((rows, HD), jnp.float32),
            VMEM((rows, HD), jnp.float32),
            VMEM((rows, width), jnp.bfloat16),
            VMEM((N_T, rows, width), jnp.bfloat16),
            VMEM((N_T, width, columns), jnp.bfloat16),
            VMEM((rows, columns), jnp.float32),
            VMEM((rows, 2 * HD), jnp.bfloat16),
            DMA((SUBS + 5,)),
            DMA((N_T,)),
            DMA((N_T - 1,)),
            DMA((N_T - 1,)),
            DMA((replicas - 1,)),
            DMA((replicas - 1,)),
            *GATHER_SEMS,
            DMA((N_T - 1,)),
            DMA((N_T - 1,)),
            DMA((15,)),
            DMA((15,)),
            DMA,
            DMA((len(BATCHES),)),
            DMA((SEEN_CHIPS, len(BATCHES))),
            DMA((SEEN_CHIPS, len(BATCHES))),
            DMA((SEEN_CHIPS + 1, len(BATCHES))),
            DMA((SEEN_CHIPS + 1, len(BATCHES))),
            DMA((SEEN_CHIPS - 1, len(BATCHES))),
        ],
        compiler_params=pltpu.CompilerParams(
            collective_id=1, has_side_effects=True, vmem_limit_bytes=58 * 2**20
        ),
        cost_estimate=pl.CostEstimate(
            flops=2 * rows * width * N_T * columns, bytes_accessed=10**8, transcendentals=10**5
        ),
    )(
        tokens,
        gain.reshape(N_T, 1, width),
        sources.reshape(1, rows),
        segments.reshape(1, rows),
        weight,
        bias,
        freqs,
        out_weight,
    )


def output_kernel(
    own_ref,
    w_ref,
    out_ref,
    buf,
    w_buf,
    total,
    ready,
    gather_send,
    gather_recv,
    w_sem,
    out_send,
    out_recv,
    own_sem,
):
    me = lax.axis_index("tensor")
    part = own_ref.shape[1] // SUBS
    others = all_others(me)
    greet(others)

    def run_of(ref, s):
        return ref.at[:, pl.ds(s * part, part)]

    gather = Gather(own_ref, buf, run_of, gather_send, gather_recv, OUT_OVER_Z)
    loads = []
    for i, t in enumerate([me] + gather.owner):
        loads.append(pltpu.make_async_copy(w_ref.at[:, t], w_buf.at[i], w_sem.at[i]))
        loads[-1].start()
    greeted(N_T - 1)
    depth = own_ref.shape[2]
    columns = total.shape[1]
    place = pl.ds(pl.multiple_of(me * columns, columns), columns)
    copies = []

    def use(kind, s):
        i = kind + 1
        if s == 0:
            loads[i].wait()
        chunk = own_ref if kind < 0 else buf.at[gather.owner[kind]]
        weight = w_buf[i].reshape(depth, columns)
        rows = chunk[:, s * part : (s + 1) * part, :].reshape(N_T * part, depth)
        term = jnp.dot(rows, weight, preferred_element_type=jnp.float32)
        term = term.astype(jnp.bfloat16).astype(jnp.float32)
        here = slice(s * N_T * part, (s + 1) * N_T * part)
        if kind < 0:
            total[here, :] = term
        else:
            total[here, :] += term

    def done(s):
        here = slice(s * N_T * part, (s + 1) * N_T * part)
        ready[s] = total[here, :].astype(jnp.bfloat16).reshape(N_T, part, columns)
        target = out_ref.at[pl.ds(s * part, part), place]
        for d, other in enumerate(others):
            copies.append(
                remote(ready.at[s, other], target, out_send.at[d, s], out_recv.at[d, s], other)
            )
            copies[-1].start()
        copies.append(pltpu.make_async_copy(ready.at[s, me], target, own_sem.at[s]))
        copies[-1].start()

    for s in range(DEPTH):
        gather.send_own(s)
    gather.run(use, done, lambda s: None)
    for copy in copies:
        copy.wait()
    gather.end()


def project_out(attended, weight):
    rows, depth = attended.shape
    columns = weight.shape[3]
    each = rows // N_T
    return pl.pallas_call(
        output_kernel,
        out_shape=jax.ShapeDtypeStruct((each, columns * N_T), jnp.bfloat16),
        in_specs=[pl.BlockSpec(memory_space=VMEM), pl.BlockSpec(memory_space=pltpu.HBM)],
        out_specs=pl.BlockSpec(memory_space=pltpu.HBM),
        scratch_shapes=[
            VMEM((N_T, N_T, each, depth), jnp.bfloat16),
            VMEM((N_T, weight.shape[0], weight.shape[2], columns), jnp.bfloat16),
            VMEM((rows, columns), jnp.float32),
            VMEM((SUBS, N_T, each // SUBS, columns), jnp.bfloat16),
            *GATHER_SEMS,
            DMA((N_T,)),
            DMA((N_T - 1, SUBS)),
            DMA((N_T - 1, SUBS)),
            DMA((SUBS,)),
        ],
        compiler_params=pltpu.CompilerParams(
            collective_id=3, has_side_effects=True, vmem_limit_bytes=48 * 2**20
        ),
        cost_estimate=pl.CostEstimate(
            flops=2 * rows * depth * N_T * columns, bytes_accessed=10**8, transcendentals=0
        ),
    )(attended.reshape(N_T, each, depth), weight)


TILE_Q = 256
SEEN_BLOCKS = 2 * SEEN_CHIPS
TILE_K = 256
LOW = -1e30


def attend_kernel(
    spots_hbm, q_hbm, kv_hbm, out_ref, starts, spots_ref, q_ref, kv_ref, load_sem, kv_sem
):
    rows = q_ref.shape[0]
    block = lax.axis_index("dp") * lax.axis_size("ctx") + lax.axis_index("ctx")
    first_row = block * rows
    loads = [
        pltpu.make_async_copy(spots_hbm, starts, load_sem.at[0]),
        pltpu.make_async_copy(spots_hbm, spots_ref, load_sem.at[1]),
        pltpu.make_async_copy(q_hbm, q_ref, load_sem.at[2]),
    ]
    for load in loads:
        load.start()

    def kv_load(back):
        return pltpu.make_async_copy(
            kv_hbm.at[block - back],
            kv_ref.at[pl.ds(pl.multiple_of((block - back) * rows, rows), rows)],
            kv_sem.at[back],
        )

    for back in range(SEEN_BLOCKS + 1):

        @pl.when(block - back >= 0)
        def _(back=back):
            kv_load(back).start()

    for load in loads:
        load.wait()
    for back in range(SEEN_BLOCKS + 1):

        @pl.when(block - back >= 0)
        def _(back=back):
            kv_load(back).wait()

    heads = q_ref.shape[1] // HD
    factor = HD**-0.5 * 1.4426950408889634
    for a in range(rows // TILE_Q):
        base = first_row + a * TILE_Q
        start = spots_ref[0:1, a * TILE_Q : (a + 1) * TILE_Q]
        query_row = base + lax.broadcasted_iota(jnp.int32, (1, TILE_Q), 1)
        low_tile = lax.div(starts[0, a * TILE_Q], TILE_K)
        high_tile = lax.div(base + TILE_Q, TILE_K)

        def one(i, carry, a=a, start=start, query_row=query_row, high_tile=high_tile):
            tile = high_tile - 1 - i
            cut = pl.ds(pl.multiple_of(tile * TILE_K, TILE_K), TILE_K)
            keys = kv_ref[cut, :HD]
            values = kv_ref[cut, HD:].T
            key_row = tile * TILE_K + lax.broadcasted_iota(jnp.int32, (TILE_K, TILE_Q), 0)
            allowed = (key_row >= start) & (key_row <= query_row)
            after = []
            for h in range(heads):
                top, denominator, weighted = carry[h]
                query = q_ref[a * TILE_Q : (a + 1) * TILE_Q, h * HD : (h + 1) * HD]
                scores = lax.dot_general(
                    keys, query, (((1,), (1,)), ((), ())), preferred_element_type=jnp.float32
                )
                scores = jnp.where(allowed, scores * factor, 2 * LOW)
                new_top = jnp.maximum(top, jnp.max(scores, axis=0, keepdims=True))
                weights = jnp.exp2(scores - new_top)
                shrink = jnp.exp2(top - new_top)
                denominator = denominator * shrink + jnp.sum(weights, axis=0, keepdims=True)
                coarse = weights.astype(jnp.bfloat16)
                fine = (weights - coarse.astype(jnp.float32)).astype(jnp.bfloat16)
                weighted = weighted * shrink
                weighted += jnp.dot(values, coarse, preferred_element_type=jnp.float32)
                weighted += jnp.dot(values, fine, preferred_element_type=jnp.float32)
                after.append((new_top, denominator, weighted))
            return tuple(after)

        begin = (
            jnp.full((1, TILE_Q), LOW, jnp.float32),
            jnp.zeros((1, TILE_Q), jnp.float32),
            jnp.zeros((HD, TILE_Q), jnp.float32),
        )
        ended = lax.fori_loop(0, high_tile - low_tile, one, (begin,) * heads)
        for h in range(heads):
            _, denominator, weighted = ended[h]
            out_ref[a * TILE_Q : (a + 1) * TILE_Q, h * HD : (h + 1) * HD] = (
                (weighted / denominator).T.astype(jnp.bfloat16)
            )


def attend(spots, queries, both):
    blocks, rows, width = both.shape
    hbm = pl.BlockSpec(memory_space=pltpu.HBM)
    return pl.pallas_call(
        attend_kernel,
        out_shape=jax.ShapeDtypeStruct(queries.shape, jnp.bfloat16),
        in_specs=[hbm, hbm, hbm],
        out_specs=pl.BlockSpec(memory_space=VMEM),
        scratch_shapes=[
            pltpu.SMEM(spots.shape, jnp.int32),
            VMEM(spots.shape, jnp.int32),
            VMEM(queries.shape, jnp.bfloat16),
            VMEM((blocks * rows, width), jnp.bfloat16),
            DMA((3,)),
            DMA((SEEN_BLOCKS + 1,)),
        ],
        compiler_params=pltpu.CompilerParams(vmem_limit_bytes=58 * 2**20),
        cost_estimate=pl.CostEstimate(flops=10**9, bytes_accessed=10**7, transcendentals=10**7),
    )(spots, queries, both)


def per_device(
    tokens, norm_gain, project_weight, project_bias, output_weight, source_row, segment_id
):
    replicas = lax.axis_size("dp") * lax.axis_size("ctx")
    flat_weight = project_weight.reshape(project_weight.shape[0], -1)
    queries, spots, both, out_columns = project(
        tokens, norm_gain, source_row, segment_id, flat_weight, project_bias, output_weight, replicas
    )
    attended = attend(spots, queries, both)
    return project_out(attended, out_columns)


def solution(mesh):
    placed = (
        P(("dp", "ctx"), "tensor"),
        P(),
        P(None, "tensor", None),
        P("tensor", None),
        P("tensor", None),
        P(("dp", "ctx")),
        P(("dp", "ctx")),
    )
    return jax.shard_map(
        per_device,
        mesh=mesh,
        in_specs=placed,
        out_specs=P(("dp", "ctx", "tensor"), None),
        check_vma=False,
    )
```

```python
import jax
import jax.numpy as jnp
import numpy as np
from jax import lax
from jax.experimental import pallas as pl
from jax.experimental.pallas import tpu as pltpu
from jax.sharding import PartitionSpec as P

HD = 128
GROUP = 4
PACK = 4096
DOC_IDS = 12
N_T = 8
SUBS = 4
DEPTH = 2
CUTS = (0, 128, 256, 384, 512)
OVER_Z = ((), ())
OUT_OVER_Z = ((1,), (2,))
BATCHES = ((0, 2), (2, 3), (3, 4))
MESH = pl.DeviceIdType.MESH
VMEM = pltpu.VMEM
DMA = pltpu.SemaphoreType.DMA


def peer(index):
    return {"tensor": index}


def greet(others):
    barrier = pltpu.get_barrier_semaphore()
    for other in others:
        pl.semaphore_signal(barrier, inc=1, device_id=peer(other), device_id_type=MESH)


def greeted(count):
    pl.semaphore_wait(pltpu.get_barrier_semaphore(), count)


def remote(src, dst, send_sem, recv_sem, to):
    return pltpu.make_async_remote_copy(
        src_ref=src,
        dst_ref=dst,
        send_sem=send_sem,
        recv_sem=recv_sem,
        device_id=peer(to),
        device_id_type=MESH,
    )


def all_others(me):
    return [lax.rem(me + d, N_T) for d in range(1, N_T)]


class Gather:
    def __init__(self, own_ref, buf, run_of, send_sem, recv_sem, over_z=((), ())):
        self.over_z = over_z
        me = lax.axis_index("tensor")
        y = lax.rem(me, 4)
        base = me - y
        self.me = me
        self.own_ref, self.buf, self.run_of = own_ref, buf, run_of
        self.send_sem, self.recv_sem = send_sem, recv_sem
        self.up = base + lax.rem(y + 1, 4)
        self.down = base + lax.rem(y + 3, 4)
        far = base + lax.rem(y + 2, 4)

        def across(t):
            return lax.rem(t + 4, N_T)

        self.pair = across(me)
        self.owner = [
            self.down,
            self.up,
            self.pair,
            far,
            across(self.down),
            across(self.up),
            across(far),
        ]
        self.started = []

    def send(self, src, owner, kind, s, to):
        copy = remote(
            self.run_of(src, s),
            self.run_of(self.buf.at[owner], s),
            self.send_sem.at[len(self.started)],
            self.recv_sem.at[kind, s],
            to,
        )
        copy.start()
        self.started.append(copy)

    def forward(self, which, kind, s, to):
        self.send(self.buf.at[self.owner[which]], self.owner[which], kind, s, to)

    def wait(self, kind, s):
        place = self.run_of(self.buf.at[self.owner[kind]], s)
        remote(place, place, self.send_sem.at[0], self.recv_sem.at[kind, s], self.pair).wait_recv()

    def send_own(self, s):
        self.send(self.own_ref, self.me, 2, s, self.pair)
        self.send(self.own_ref, self.me, 0, s, self.up)
        self.send(self.own_ref, self.me, 1, s, self.down)

    def run(self, use, done, between):
        for s in range(SUBS):
            self.wait(0, s)
            if s % 2 == 0:
                self.forward(0, 3, s, self.up)
            if s in self.over_z[0]:
                self.forward(0, 4, s, self.pair)
            self.wait(1, s)
            if s % 2 == 1:
                self.forward(1, 3, s, self.down)
            if s in self.over_z[1]:
                self.forward(1, 5, s, self.pair)
            self.wait(2, s)
            if s not in self.over_z[0]:
                self.forward(2, 4, s, self.up)
            if s not in self.over_z[1]:
                self.forward(2, 5, s, self.down)
            if s + DEPTH < SUBS:
                self.send_own(s + DEPTH)
            for kind in (-1, 0, 1, 2):
                use(kind, s)
            if s > 0:
                self.across_sides(s - 1, use)
            self.wait(3, s)
            self.forward(3, 6, s, self.pair)
            use(3, s)
            between(s)
            if s > 0:
                self.last(s - 1, use, done)
        self.across_sides(SUBS - 1, use)
        self.last(SUBS - 1, use, done)

    def across_sides(self, s, use):
        self.wait(4, s)
        use(4, s)
        self.wait(5, s)
        use(5, s)

    def last(self, s, use, done):
        self.wait(6, s)
        use(6, s)
        done(s)

    def end(self):
        for copy in self.started:
            copy.wait_send()


GATHER_SEMS = [DMA((7 * SUBS,)), DMA((7, SUBS))]
SEEN_CHIPS = 4


def put(src, dst, send_sem, recv_sem, to):
    return pltpu.make_async_remote_copy(
        src_ref=src,
        dst_ref=dst,
        send_sem=send_sem,
        recv_sem=recv_sem,
        device_id=to,
        device_id_type=MESH,
    )


def ring_of(replica):
    per = lax.axis_size("ctx")
    return {"dp": lax.div(replica, per), "ctx": lax.rem(replica, per)}


class Columns:
    def __init__(self, w_ref, all_ref, a2a_send, a2a_recv, send_sem, recv_sem, own_sem):
        self.all_ref = all_ref
        self.a2a_send, self.a2a_recv = a2a_send, a2a_recv
        self.send_sem, self.recv_sem = send_sem, recv_sem
        self.own_sem = own_sem
        self.w_ref = w_ref
        self.me = lax.axis_index("tensor")
        per = lax.axis_size("ctx")
        dp, ctx = lax.axis_index("dp"), lax.axis_index("ctx")
        core = lax.rem(ctx, 2)
        self.replica = dp * per + ctx
        sibling = ctx + 1 - 2 * core
        up, down, far = lax.rem(ctx + 2, per), lax.rem(ctx + per - 2, per), lax.rem(ctx + 4, per)
        here, there = dp * per, (1 - dp) * per
        self.to = {
            "z": {"dp": 1 - dp},
            "up": {"ctx": up},
            "down": {"ctx": down},
            "near": {"ctx": sibling},
        }
        self.piece = {
            "own": here + ctx,
            "z": there + ctx,
            "down": here + down,
            "up": here + up,
            "z down": there + down,
            "z up": there + up,
            "far": here + far,
            "z far": there + far,
        }
        self.near_piece = {}
        for name, index in self.piece.items():
            self.near_piece[name] = index + 1 - 2 * core
        self.started = []

    def block(self, t):
        piece, columns = self.all_ref.shape[2:]
        rows = pl.ds(pl.multiple_of(self.replica * piece, piece), piece)
        return self.w_ref.at[rows, pl.ds(pl.multiple_of(t * columns, columns), columns)]

    def fetch(self):
        place = self.all_ref.at[self.replica, self.me]
        self.own = pltpu.make_async_copy(self.block(self.me), place, self.own_sem)
        self.own.start()
        self.fetches = []
        for d, other in enumerate(all_others(self.me)):
            copy = remote(self.block(other), place, self.a2a_send.at[d], self.a2a_recv.at[d], other)
            copy.start()
            self.fetches.append(copy)

    def send(self, name, way, arrives):
        place = self.all_ref.at[self.piece[name]]
        copy = put(
            place,
            place,
            self.send_sem.at[len(self.started)],
            self.recv_sem.at[arrives],
            self.to[way],
        )
        copy.start()
        self.started.append(copy)

    def wait(self, index, arrives):
        place = self.all_ref.at[index]
        put(
            place, place, self.send_sem.at[0], self.recv_sem.at[arrives], self.to["near"]
        ).wait_recv()

    ARRIVES = ("z", "down", "up", "z down", "z up", "far", "z far")

    def arrived(self, name):
        self.wait(self.piece[name], self.ARRIVES.index(name))
        self.send_near(name)

    def send_near(self, name):
        self.send(name, "near", 7 + list(self.piece).index(name))

    def step(self, s):
        if s == 0:
            self.own.wait()
            for copy in self.fetches:
                copy.wait()
            self.send("own", "z", 0)
            self.send("own", "up", 1)
            self.send("own", "down", 2)
            self.send_near("own")
        if s == 1:
            self.arrived("z")
            self.send("z", "up", 3)
            self.send("z", "down", 4)
        if s == 2:
            self.arrived("down")
            self.send("down", "up", 5)
            self.arrived("up")
        if s == 3:
            self.arrived("z up")
            self.send("z up", "down", 6)
            self.arrived("z down")
            self.arrived("far")

    def last(self):
        self.arrived("z far")

    def end(self):
        for i, name in enumerate(self.piece):
            self.wait(self.near_piece[name], 7 + i)
        for copy in self.started:
            copy.wait_send()


class Shared:
    def __init__(self, own, kv_ref, own_sem, send_sem, recv_sem, near_send, near_recv, along_send):
        per = lax.axis_size("ctx") // 2
        ctx = lax.axis_index("ctx")
        self.per = per
        self.core = lax.rem(ctx, 2)
        self.chip = lax.axis_index("dp") * per + lax.div(ctx, 2)
        self.chips = lax.axis_size("dp") * per
        self.block = self.chip * 2 + self.core
        self.sibling = {"ctx": ctx + 1 - 2 * self.core}
        self.sibling_block = self.block + 1 - 2 * self.core
        self.own, self.kv_ref, self.own_sem = own, kv_ref, own_sem
        self.send_sem, self.recv_sem = send_sem, recv_sem
        self.near_send, self.near_recv = near_send, near_recv
        self.along_send = along_send
        self.x = lax.rem(self.chip, per)

    def run(self, ref, s):
        first, last = (CUTS[cut] for cut in BATCHES[s])
        return ref.at[pl.ds(first, last - first)]

    def to_chip(self, k, s):
        other = self.chip + k
        return put(
            self.run(self.own, s),
            self.run(self.kv_ref.at[self.block], s),
            self.send_sem.at[k - 1, s],
            self.recv_sem.at[k - 1, s],
            {"dp": lax.div(other, self.per), "ctx": lax.rem(other, self.per) * 2 + self.core},
        )

    def to_sibling(self, k, s):
        place = self.run(self.kv_ref.at[self.block - 2 * k], s)
        return put(
            self.run(self.own, s) if k == 0 else place,
            place,
            self.near_send.at[k, s],
            self.near_recv.at[k, s],
            self.sibling,
        )

    def keep(self, s):
        return pltpu.make_async_copy(
            self.run(self.own, s), self.run(self.kv_ref.at[self.block], s), self.own_sem.at[s]
        )

    def sends(self, act):
        for k in (2, 1, 3):

            @pl.when(self.x + k < self.per)
            def _(k=k):
                act(k)

        @pl.when(self.chip + self.per < self.chips)
        def _():
            act(self.per)

    def send(self, s):
        self.sends(lambda k: self.to_chip(k, s).start())
        self.to_sibling(0, s).start()
        self.keep(s).start()

    def along(self, m, s):
        place = self.run(self.kv_ref.at[self.block - 2 * self.per], s)
        return put(
            place,
            place,
            self.along_send.at[m - 1, s],
            self.recv_sem.at[self.per - m - 1, s],
            {"ctx": (self.x - m) * 2 + self.core},
        )

    def relays(self, act):
        for m in (2, 1, 3):

            @pl.when((self.chip >= self.per) & (self.x >= m))
            def _(m=m):
                act(m)

    def pass_on(self, s):
        for k in (4, 1, 3, 2):

            @pl.when(self.chip - k >= 0)
            def _(k=k):
                place = self.run(self.kv_ref.at[self.block - 2 * k], s)
                put(
                    place,
                    place,
                    self.send_sem.at[k - 1, s],
                    self.recv_sem.at[k - 1, s],
                    self.sibling,
                ).wait_recv()

            if k == self.per:
                self.relays(lambda m: self.along(m, s).start())

            @pl.when(self.chip - k >= 0)
            def _(k=k):
                self.to_sibling(k, s).start()

    def from_sibling(self, k, s):
        place = self.run(self.kv_ref.at[self.sibling_block - 2 * k], s)
        put(
            place, place, self.near_send.at[k, s], self.near_recv.at[k, s], self.sibling
        ).wait_recv()

    def end(self):
        for s in range(len(BATCHES)):
            self.keep(s).wait()
            self.to_sibling(0, s).wait_send()
            self.from_sibling(0, s)
        for k in range(1, SEEN_CHIPS + 1):

            @pl.when(self.chip - k >= 0)
            def _(k=k):
                for s in range(len(BATCHES)):
                    self.to_sibling(k, s).wait_send()
                    self.from_sibling(k, s)

        for s in range(len(BATCHES)):
            self.sends(lambda k, s=s: self.to_chip(k, s).wait_send())
            self.relays(lambda m, s=s: self.along(m, s).wait_send())


def project_kernel(
    tok_hbm,
    gain_hbm,
    source_hbm,
    segment_hbm,
    w_ref,
    bias_hbm,
    freq_hbm,
    wo_ref,
    q_ref,
    spots_ref,
    kv_ref,
    columns_ref,
    tok,
    gain_rows,
    sources_row,
    segments_row,
    bias_row,
    freq_row,
    stats,
    docs,
    scales,
    cosines,
    sines,
    normed,
    buf,
    w_buf,
    total,
    own,
    load_sem,
    w_sem,
    stat_send,
    stat_recv,
    doc_send,
    doc_recv,
    gather_send,
    gather_recv,
    a2a_send,
    a2a_recv,
    col_send,
    col_recv,
    col_own,
    kv_own,
    kv_send,
    kv_recv,
    near_send,
    near_recv,
    along_send,
):
    me = lax.axis_index("tensor")
    replica = lax.axis_index("dp") * lax.axis_size("ctx") + lax.axis_index("ctx")
    replicas = docs.shape[0]
    rows, width = tok.shape
    features = width * N_T
    step = rows // SUBS
    others = all_others(me)
    alike = [ring_of(lax.rem(replica + d, replicas)) for d in range(1, replicas)]
    greet(others)
    for other in alike:
        pl.semaphore_signal(
            pltpu.get_barrier_semaphore(), inc=1, device_id=other, device_id_type=MESH
        )
    small = []
    for i, (src, dst) in enumerate(
        (
            (source_hbm, sources_row),
            (segment_hbm, segments_row),
            (gain_hbm, gain_rows),
            (bias_hbm, bias_row),
            (freq_hbm, freq_row),
        )
    ):
        small.append(pltpu.make_async_copy(src, dst, load_sem.at[SUBS + i]))
        small[-1].start()
    token_loads = []
    for i in range(SUBS):
        cut = pl.ds(i * step, step)
        token_loads.append(pltpu.make_async_copy(tok_hbm.at[cut], tok.at[cut], load_sem.at[i]))
        token_loads[-1].start()

    def run_of(ref, s):
        return ref.at[pl.ds(CUTS[s], CUTS[s + 1] - CUTS[s])]

    gather = Gather(tok, buf, run_of, gather_send, gather_recv, OVER_Z)
    w_loads = []
    for i, t in enumerate([me] + gather.owner):
        w_loads.append(
            pltpu.make_async_copy(
                w_ref.at[pl.ds(pl.multiple_of(t * width, width), width)], w_buf.at[i], w_sem.at[i]
            )
        )
        w_loads[-1].start()

    for copy in small:
        copy.wait()
    sources = sources_row[...]
    segments = segments_row[...]
    row = replica * rows + lax.broadcasted_iota(jnp.int32, (1, rows), 1)
    none = rows * replicas
    lane = lax.broadcasted_iota(jnp.int32, (8, 128), 1)
    line = lax.broadcasted_iota(jnp.int32, (8, 128), 0)
    table = jnp.full((8, 128), none, jnp.int32)
    for doc in range(DOC_IDS):
        of_doc = segments == doc
        first_source = jnp.min(jnp.where(of_doc, sources, none), axis=1, keepdims=True)
        first_packed = jnp.min(jnp.where(of_doc, row, none), axis=1, keepdims=True)
        found = jnp.where(line == 0, first_source, first_packed)
        table = jnp.where(lane == doc, found, table)
    docs[pl.ds(replica, 1)] = table[None]
    for i in range(SUBS):
        token_loads[i].wait()
        squares = jnp.zeros((step, 128), jnp.float32)
        for j in range(width // 128):
            part = tok[i * step : (i + 1) * step, j * 128 : (j + 1) * 128].astype(jnp.float32)
            squares = squares + part * part
        summed = jnp.sum(squares.T, axis=0, keepdims=True)
        stats[pl.ds(me, 1), :, i * step : (i + 1) * step] = jnp.broadcast_to(
            summed[None], (1, 8, step)
        )
    greeted(N_T - 1 + replicas - 1)

    stat_copies = []
    for d, other in enumerate(others):
        stat_copies.append(
            remote(stats.at[me], stats.at[me], stat_send.at[d], stat_recv.at[d], other)
        )
        stat_copies[-1].start()
    doc_copies = []
    for d, other in enumerate(alike):
        place = docs.at[replica]
        doc_copies.append(put(place, place, doc_send.at[d], doc_recv.at[d], other))
        doc_copies[-1].start()
    for s in range(DEPTH):
        gather.send_own(s)
    columns = Columns(wo_ref, columns_ref, a2a_send, a2a_recv, col_send, col_recv, col_own)
    columns.fetch()
    for copy in stat_copies:
        copy.wait()
    summed = stats[0]
    for t in range(1, N_T):
        summed = summed + stats[t]
    scale = lax.rsqrt(summed[0:1] * (1.0 / features) + 1e-06)
    for i in range(SUBS):
        here = slice(i * step, (i + 1) * step)
        scales[here, :] = jnp.broadcast_to(scale[:, here], (128, step)).T

    shared = Shared(own, kv_ref, kv_own, kv_send, kv_recv, near_send, near_recv, along_send)
    def find_spots():
        for copy in doc_copies:
            copy.wait()
        table = docs[0]
        for r in range(1, replicas):
            table = jnp.minimum(table, docs[r])
        start = jnp.full((1, rows), -1, jnp.int32)
        place = row
        for doc in range(DOC_IDS):
            first_source = table[0:1, doc : doc + 1]
            first_packed = table[1:2, doc : doc + 1]
            later = (first_source <= row) & (first_source > start)
            start = jnp.where(later, first_source, start)
            place = jnp.where(later, row + (first_packed - first_source), place)
        spots_ref[...] = jnp.where(
            lax.broadcasted_iota(jnp.int32, (8, rows), 0) == 0, start, place
        )
        position = lax.rem(place, PACK).astype(jnp.float32)
        first = lax.broadcasted_iota(jnp.int32, (step, HD), 1) < HD // 2
        for i in range(SUBS):
            here = slice(i * step, (i + 1) * step)
            angle = jnp.broadcast_to(position[:, here], (128, step)).T * freq_row[...]
            cosines[here, :] = jnp.cos(angle)
            sine = jnp.sin(angle)
            sines[here, :] = jnp.where(first, -sine, sine)

    def use(kind, s):
        i = kind + 1
        if s == 0:
            w_loads[i].wait()
        owner = me if kind < 0 else gather.owner[kind]
        chunk = tok if kind < 0 else buf.at[owner]
        here = slice(CUTS[s], CUTS[s + 1])
        along = scales[here, :]
        for j in range(width // 128):
            cut = slice(j * 128, (j + 1) * 128)
            wide = chunk[here, cut].astype(jnp.float32)
            normed[here, cut] = (wide * along * gain_rows[owner, :, cut]).astype(jnp.bfloat16)
        term = jnp.dot(normed[here, :], w_buf[i], preferred_element_type=jnp.float32)
        if kind < 0:
            total[here, :] = term
        else:
            total[here, :] += term

    def done(s):
        here = slice(CUTS[s], CUTS[s + 1])
        bias = bias_row[...].astype(jnp.float32)
        cosine = cosines[here, :]
        sine = sines[here, :]

        def slot(index):
            cut = slice(index * HD, (index + 1) * HD)
            return (total[here, cut] + bias[:, cut]).astype(jnp.bfloat16)

        def turned(index):
            wide = slot(index).astype(jnp.float32)
            return (wide * cosine + pltpu.roll(wide, HD // 2, 1) * sine).astype(jnp.bfloat16)

        own[here, :HD] = turned(GROUP)
        own[here, HD:] = slot(GROUP + 1)
        for batch, (_, end) in enumerate(BATCHES):
            if end == s + 1:
                shared.send(batch)
        for head in range(GROUP):
            q_ref[here, head * HD : (head + 1) * HD] = turned(head)

    find_spots()
    gather.run(use, done, columns.step)
    shared.pass_on(0)
    shared.pass_on(1)
    columns.last()
    shared.pass_on(2)
    columns.end()
    shared.end()
    gather.end()


def project(tokens, gain, sources, segments, weight, bias, out_weight, replicas):
    rows, width = tokens.shape
    columns = weight.shape[1]
    depth, out_width = out_weight.shape
    half = HD // 2
    freqs = (1e6 ** (-(np.arange(half) * 2.0) / HD)).astype(np.float32)
    freqs = jnp.asarray(np.concatenate([freqs, freqs])[None])
    hbm = pl.BlockSpec(memory_space=pltpu.HBM)
    vmem = pl.BlockSpec(memory_space=VMEM)
    return pl.pallas_call(
        project_kernel,
        out_shape=(
            jax.ShapeDtypeStruct((rows, GROUP * HD), jnp.bfloat16),
            jax.ShapeDtypeStruct((8, rows), jnp.int32),
            jax.ShapeDtypeStruct((replicas, rows, 2 * HD), jnp.bfloat16),
            jax.ShapeDtypeStruct((replicas, N_T, depth // replicas, out_width // N_T), jnp.bfloat16),
        ),
        in_specs=[hbm] * 8,
        out_specs=(vmem, vmem, hbm, hbm),
        scratch_shapes=[
            VMEM((rows, width), jnp.bfloat16),
            VMEM((N_T, 1, width), jnp.float32),
            VMEM((1, rows), jnp.int32),
            VMEM((1, rows), jnp.int32),
            VMEM((1, columns), jnp.bfloat16),
            VMEM((1, HD), jnp.float32),
            VMEM((N_T, 8, rows), jnp.float32),
            VMEM((replicas, 8, 128), jnp.int32),
            VMEM((rows, HD), jnp.float32),
            VMEM((rows, HD), jnp.float32),
            VMEM((rows, HD), jnp.float32),
            VMEM((rows, width), jnp.bfloat16),
            VMEM((N_T, rows, width), jnp.bfloat16),
            VMEM((N_T, width, columns), jnp.bfloat16),
            VMEM((rows, columns), jnp.float32),
            VMEM((rows, 2 * HD), jnp.bfloat16),
            DMA((SUBS + 5,)),
            DMA((N_T,)),
            DMA((N_T - 1,)),
            DMA((N_T - 1,)),
            DMA((replicas - 1,)),
            DMA((replicas - 1,)),
            *GATHER_SEMS,
            DMA((N_T - 1,)),
            DMA((N_T - 1,)),
            DMA((15,)),
            DMA((15,)),
            DMA,
            DMA((len(BATCHES),)),
            DMA((SEEN_CHIPS, len(BATCHES))),
            DMA((SEEN_CHIPS, len(BATCHES))),
            DMA((SEEN_CHIPS + 1, len(BATCHES))),
            DMA((SEEN_CHIPS + 1, len(BATCHES))),
            DMA((SEEN_CHIPS - 1, len(BATCHES))),
        ],
        compiler_params=pltpu.CompilerParams(
            collective_id=1, has_side_effects=True, vmem_limit_bytes=58 * 2**20
        ),
        cost_estimate=pl.CostEstimate(
            flops=2 * rows * width * N_T * columns, bytes_accessed=10**8, transcendentals=10**5
        ),
    )(
        tokens,
        gain.reshape(N_T, 1, width),
        sources.reshape(1, rows),
        segments.reshape(1, rows),
        weight,
        bias,
        freqs,
        out_weight,
    )


def output_kernel(
    own_hbm,
    w_ref,
    out_ref,
    own_ref,
    buf,
    w_buf,
    total,
    ready,
    gather_send,
    gather_recv,
    w_sem,
    out_send,
    out_recv,
    own_sem,
):
    me = lax.axis_index("tensor")
    part = own_ref.shape[1] // SUBS
    others = all_others(me)
    greet(others)
    load_own = pltpu.make_async_copy(own_hbm, own_ref, own_sem.at[SUBS])
    load_own.start()

    def run_of(ref, s):
        return ref.at[:, pl.ds(s * part, part)]

    gather = Gather(own_ref, buf, run_of, gather_send, gather_recv, OUT_OVER_Z)
    loads = []
    for i, t in enumerate([me] + gather.owner):
        loads.append(pltpu.make_async_copy(w_ref.at[:, t], w_buf.at[i], w_sem.at[i]))
        loads[-1].start()
    load_own.wait()
    greeted(N_T - 1)
    depth = own_ref.shape[2]
    columns = total.shape[1]
    place = pl.ds(pl.multiple_of(me * columns, columns), columns)
    copies = []

    def use(kind, s):
        i = kind + 1
        if s == 0:
            loads[i].wait()
        chunk = own_ref if kind < 0 else buf.at[gather.owner[kind]]
        weight = w_buf[i].reshape(depth, columns)
        rows = chunk[:, s * part : (s + 1) * part, :].reshape(N_T * part, depth)
        term = jnp.dot(rows, weight, preferred_element_type=jnp.float32)
        term = term.astype(jnp.bfloat16).astype(jnp.float32)
        here = slice(s * N_T * part, (s + 1) * N_T * part)
        if kind < 0:
            total[here, :] = term
        else:
            total[here, :] += term

    def done(s):
        here = slice(s * N_T * part, (s + 1) * N_T * part)
        ready[s] = total[here, :].astype(jnp.bfloat16).reshape(N_T, part, columns)
        target = out_ref.at[pl.ds(s * part, part), place]
        for d, other in enumerate(others):
            copies.append(
                remote(ready.at[s, other], target, out_send.at[d, s], out_recv.at[d, s], other)
            )
            copies[-1].start()
        copies.append(pltpu.make_async_copy(ready.at[s, me], target, own_sem.at[s]))
        copies[-1].start()

    for s in range(DEPTH):
        gather.send_own(s)
    gather.run(use, done, lambda s: None)
    for copy in copies:
        copy.wait()
    gather.end()


def project_out(attended, weight):
    rows, depth = attended.shape
    columns = weight.shape[3]
    each = rows // N_T
    return pl.pallas_call(
        output_kernel,
        out_shape=jax.ShapeDtypeStruct((each, columns * N_T), jnp.bfloat16),
        in_specs=[pl.BlockSpec(memory_space=pltpu.HBM), pl.BlockSpec(memory_space=pltpu.HBM)],
        out_specs=pl.BlockSpec(memory_space=pltpu.HBM),
        scratch_shapes=[
            VMEM((N_T, each, depth), jnp.bfloat16),
            VMEM((N_T, N_T, each, depth), jnp.bfloat16),
            VMEM((N_T, weight.shape[0], weight.shape[2], columns), jnp.bfloat16),
            VMEM((rows, columns), jnp.float32),
            VMEM((SUBS, N_T, each // SUBS, columns), jnp.bfloat16),
            *GATHER_SEMS,
            DMA((N_T,)),
            DMA((N_T - 1, SUBS)),
            DMA((N_T - 1, SUBS)),
            DMA((SUBS + 1,)),
        ],
        compiler_params=pltpu.CompilerParams(
            collective_id=3, has_side_effects=True, vmem_limit_bytes=48 * 2**20
        ),
        cost_estimate=pl.CostEstimate(
            flops=2 * rows * depth * N_T * columns, bytes_accessed=10**8, transcendentals=0
        ),
    )(attended.reshape(N_T, each, depth), weight)


TILE_Q = 256
SEEN_BLOCKS = 2 * SEEN_CHIPS
TILE_K = 256
LOW = -1e30


def attend_kernel(
    spots_hbm, q_hbm, kv_hbm, out_ref, starts, spots_ref, q_ref, kv_ref, load_sem, kv_sem
):
    rows = q_ref.shape[0]
    block = lax.axis_index("dp") * lax.axis_size("ctx") + lax.axis_index("ctx")
    first_row = block * rows
    loads = [
        pltpu.make_async_copy(spots_hbm, starts, load_sem.at[0]),
        pltpu.make_async_copy(spots_hbm, spots_ref, load_sem.at[1]),
        pltpu.make_async_copy(q_hbm, q_ref, load_sem.at[2]),
    ]
    for load in loads:
        load.start()

    def kv_load(back):
        return pltpu.make_async_copy(
            kv_hbm.at[block - back],
            kv_ref.at[pl.ds(pl.multiple_of((block - back) * rows, rows), rows)],
            kv_sem.at[back],
        )

    for back in range(SEEN_BLOCKS + 1):

        @pl.when(block - back >= 0)
        def _(back=back):
            kv_load(back).start()

    for load in loads:
        load.wait()
    for back in range(SEEN_BLOCKS + 1):

        @pl.when(block - back >= 0)
        def _(back=back):
            kv_load(back).wait()

    heads = q_ref.shape[1] // HD
    factor = HD**-0.5 * 1.4426950408889634
    for a in range(rows // TILE_Q):
        base = first_row + a * TILE_Q
        start = spots_ref[0:1, a * TILE_Q : (a + 1) * TILE_Q]
        query_row = base + lax.broadcasted_iota(jnp.int32, (1, TILE_Q), 1)
        low_tile = lax.div(starts[0, a * TILE_Q], TILE_K)
        high_tile = lax.div(base + TILE_Q, TILE_K)

        def one(tile, carry, masked, a=a, start=start, query_row=query_row):
            cut = pl.ds(pl.multiple_of(tile * TILE_K, TILE_K), TILE_K)
            keys = kv_ref[cut, :HD]
            values = kv_ref[cut, HD:].T
            if masked:
                key_row = tile * TILE_K + lax.broadcasted_iota(jnp.int32, (TILE_K, TILE_Q), 0)
                allowed = (key_row >= start) & (key_row <= query_row)
            after = []
            for h in range(heads):
                top, denominator, weighted = carry[h]
                query = q_ref[a * TILE_Q : (a + 1) * TILE_Q, h * HD : (h + 1) * HD]
                scores = lax.dot_general(
                    keys, query, (((1,), (1,)), ((), ())), preferred_element_type=jnp.float32
                )
                scores = scores * factor
                if masked:
                    scores = jnp.where(allowed, scores, 2 * LOW)
                new_top = jnp.maximum(top, jnp.max(scores, axis=0, keepdims=True))
                weights = jnp.exp2(scores - new_top)
                shrink = jnp.exp2(top - new_top)
                denominator = denominator * shrink + jnp.sum(weights, axis=0, keepdims=True)
                coarse = weights.astype(jnp.bfloat16)
                fine = (weights - coarse.astype(jnp.float32)).astype(jnp.bfloat16)
                weighted = weighted * shrink
                weighted += jnp.dot(values, coarse, preferred_element_type=jnp.float32)
                weighted += jnp.dot(values, fine, preferred_element_type=jnp.float32)
                after.append((new_top, denominator, weighted))
            return tuple(after)

        full_tile = jnp.minimum(
            lax.div(starts[0, (a + 1) * TILE_Q - 1] + TILE_K - 1, TILE_K), high_tile - 1
        )
        begin = (
            jnp.full((1, TILE_Q), LOW, jnp.float32),
            jnp.zeros((1, TILE_Q), jnp.float32),
            jnp.zeros((HD, TILE_Q), jnp.float32),
        )
        ended = one(high_tile - 1, (begin,) * heads, True)
        ended = lax.fori_loop(
            full_tile, high_tile - 1, lambda t, carry: one(t, carry, False), ended
        )
        ended = lax.fori_loop(low_tile, full_tile, lambda t, carry: one(t, carry, True), ended)
        for h in range(heads):
            _, denominator, weighted = ended[h]
            out_ref[a * TILE_Q : (a + 1) * TILE_Q, h * HD : (h + 1) * HD] = (
                (weighted / denominator).T.astype(jnp.bfloat16)
            )


def attend(spots, queries, both):
    blocks, rows, width = both.shape
    hbm = pl.BlockSpec(memory_space=pltpu.HBM)
    return pl.pallas_call(
        attend_kernel,
        out_shape=jax.ShapeDtypeStruct(queries.shape, jnp.bfloat16),
        in_specs=[hbm, hbm, hbm],
        out_specs=pl.BlockSpec(memory_space=VMEM),
        scratch_shapes=[
            pltpu.SMEM(spots.shape, jnp.int32),
            VMEM(spots.shape, jnp.int32),
            VMEM(queries.shape, jnp.bfloat16),
            VMEM((blocks * rows, width), jnp.bfloat16),
            DMA((3,)),
            DMA((SEEN_BLOCKS + 1,)),
        ],
        compiler_params=pltpu.CompilerParams(vmem_limit_bytes=58 * 2**20),
        cost_estimate=pl.CostEstimate(flops=10**9, bytes_accessed=10**7, transcendentals=10**7),
    )(spots, queries, both)


def per_device(
    tokens, norm_gain, project_weight, project_bias, output_weight, source_row, segment_id
):
    replicas = lax.axis_size("dp") * lax.axis_size("ctx")
    flat_weight = project_weight.reshape(project_weight.shape[0], -1)
    queries, spots, both, out_columns = project(
        tokens, norm_gain, source_row, segment_id, flat_weight, project_bias, output_weight, replicas
    )
    attended = attend(spots, queries, both)
    return project_out(attended, out_columns)


def solution(mesh):
    placed = (
        P(("dp", "ctx"), "tensor"),
        P(),
        P(None, "tensor", None),
        P("tensor", None),
        P("tensor", None),
        P(("dp", "ctx")),
        P(("dp", "ctx")),
    )
    return jax.shard_map(
        per_device,
        mesh=mesh,
        in_specs=placed,
        out_specs=P(("dp", "ctx", "tensor"), None),
        check_vma=False,
    )
```

```python
import jax
import jax.numpy as jnp
import numpy as np
from jax import lax
from jax.experimental import pallas as pl
from jax.experimental.pallas import tpu as pltpu
from jax.sharding import PartitionSpec as P

HD = 128
GROUP = 4
PACK = 4096
DOC_IDS = 12
N_T = 8
SUBS = 4
DEPTH = 2
CUTS = (0, 128, 256, 384, 512)
OVER_Z = ((), ())
OUT_OVER_Z = ((1,), (2,))
BATCHES = ((0, 2), (2, 3), (3, 4))
MESH = pl.DeviceIdType.MESH
VMEM = pltpu.VMEM
DMA = pltpu.SemaphoreType.DMA


def peer(index):
    return {"tensor": index}


def greet(others):
    barrier = pltpu.get_barrier_semaphore()
    for other in others:
        pl.semaphore_signal(barrier, inc=1, device_id=peer(other), device_id_type=MESH)


def greeted(count):
    pl.semaphore_wait(pltpu.get_barrier_semaphore(), count)


def remote(src, dst, send_sem, recv_sem, to):
    return pltpu.make_async_remote_copy(
        src_ref=src,
        dst_ref=dst,
        send_sem=send_sem,
        recv_sem=recv_sem,
        device_id=peer(to),
        device_id_type=MESH,
    )


def all_others(me):
    return [lax.rem(me + d, N_T) for d in range(1, N_T)]


class Gather:
    def __init__(self, own_ref, buf, run_of, send_sem, recv_sem, over_z=((), ())):
        self.over_z = over_z
        me = lax.axis_index("tensor")
        y = lax.rem(me, 4)
        base = me - y
        self.me = me
        self.own_ref, self.buf, self.run_of = own_ref, buf, run_of
        self.send_sem, self.recv_sem = send_sem, recv_sem
        self.up = base + lax.rem(y + 1, 4)
        self.down = base + lax.rem(y + 3, 4)
        far = base + lax.rem(y + 2, 4)

        def across(t):
            return lax.rem(t + 4, N_T)

        self.pair = across(me)
        self.owner = [
            self.down,
            self.up,
            self.pair,
            far,
            across(self.down),
            across(self.up),
            across(far),
        ]
        self.started = []

    def send(self, src, owner, kind, s, to):
        copy = remote(
            self.run_of(src, s),
            self.run_of(self.buf.at[owner], s),
            self.send_sem.at[len(self.started)],
            self.recv_sem.at[kind, s],
            to,
        )
        copy.start()
        self.started.append(copy)

    def forward(self, which, kind, s, to):
        self.send(self.buf.at[self.owner[which]], self.owner[which], kind, s, to)

    def wait(self, kind, s):
        place = self.run_of(self.buf.at[self.owner[kind]], s)
        remote(place, place, self.send_sem.at[0], self.recv_sem.at[kind, s], self.pair).wait_recv()

    def send_own(self, s):
        self.send(self.own_ref, self.me, 2, s, self.pair)
        self.send(self.own_ref, self.me, 0, s, self.up)
        self.send(self.own_ref, self.me, 1, s, self.down)

    def run(self, use, done, between):
        for s in range(SUBS):
            self.wait(0, s)
            if s % 2 == 0:
                self.forward(0, 3, s, self.up)
            if s in self.over_z[0]:
                self.forward(0, 4, s, self.pair)
            self.wait(1, s)
            if s % 2 == 1:
                self.forward(1, 3, s, self.down)
            if s in self.over_z[1]:
                self.forward(1, 5, s, self.pair)
            self.wait(2, s)
            if s not in self.over_z[0]:
                self.forward(2, 4, s, self.up)
            if s not in self.over_z[1]:
                self.forward(2, 5, s, self.down)
            if s + DEPTH < SUBS:
                self.send_own(s + DEPTH)
            for kind in (-1, 0, 1, 2):
                use(kind, s)
            if s > 0:
                self.across_sides(s - 1, use)
            self.wait(3, s)
            self.forward(3, 6, s, self.pair)
            use(3, s)
            if s > 0:
                self.last(s - 1, use, done)
            between(s)
        self.across_sides(SUBS - 1, use)
        self.last(SUBS - 1, use, done)

    def across_sides(self, s, use):
        self.wait(4, s)
        use(4, s)
        self.wait(5, s)
        use(5, s)

    def last(self, s, use, done):
        self.wait(6, s)
        use(6, s)
        done(s)

    def end(self):
        for copy in self.started:
            copy.wait_send()


GATHER_SEMS = [DMA((7 * SUBS,)), DMA((7, SUBS))]
SEEN_CHIPS = 4


def put(src, dst, send_sem, recv_sem, to):
    return pltpu.make_async_remote_copy(
        src_ref=src,
        dst_ref=dst,
        send_sem=send_sem,
        recv_sem=recv_sem,
        device_id=to,
        device_id_type=MESH,
    )


def ring_of(replica):
    per = lax.axis_size("ctx")
    return {"dp": lax.div(replica, per), "ctx": lax.rem(replica, per)}


class Columns:
    def __init__(self, w_ref, all_ref, a2a_send, a2a_recv, send_sem, recv_sem, own_sem):
        self.all_ref = all_ref
        self.a2a_send, self.a2a_recv = a2a_send, a2a_recv
        self.send_sem, self.recv_sem = send_sem, recv_sem
        self.own_sem = own_sem
        self.w_ref = w_ref
        self.me = lax.axis_index("tensor")
        per = lax.axis_size("ctx")
        dp, ctx = lax.axis_index("dp"), lax.axis_index("ctx")
        core = lax.rem(ctx, 2)
        self.replica = dp * per + ctx
        sibling = ctx + 1 - 2 * core
        up, down, far = lax.rem(ctx + 2, per), lax.rem(ctx + per - 2, per), lax.rem(ctx + 4, per)
        here, there = dp * per, (1 - dp) * per
        self.to = {
            "z": {"dp": 1 - dp},
            "up": {"ctx": up},
            "down": {"ctx": down},
            "near": {"ctx": sibling},
        }
        self.piece = {
            "own": here + ctx,
            "z": there + ctx,
            "down": here + down,
            "up": here + up,
            "z down": there + down,
            "z up": there + up,
            "far": here + far,
            "z far": there + far,
        }
        self.near_piece = {}
        for name, index in self.piece.items():
            self.near_piece[name] = index + 1 - 2 * core
        self.started = []

    def block(self, t):
        piece, columns = self.all_ref.shape[2:]
        rows = pl.ds(pl.multiple_of(self.replica * piece, piece), piece)
        return self.w_ref.at[rows, pl.ds(pl.multiple_of(t * columns, columns), columns)]

    def fetch(self):
        place = self.all_ref.at[self.replica, self.me]
        self.own = pltpu.make_async_copy(self.block(self.me), place, self.own_sem)
        self.own.start()
        self.fetches = []
        for d, other in enumerate(all_others(self.me)):
            copy = remote(self.block(other), place, self.a2a_send.at[d], self.a2a_recv.at[d], other)
            copy.start()
            self.fetches.append(copy)

    def send(self, name, way, arrives):
        place = self.all_ref.at[self.piece[name]]
        copy = put(
            place,
            place,
            self.send_sem.at[len(self.started)],
            self.recv_sem.at[arrives],
            self.to[way],
        )
        copy.start()
        self.started.append(copy)

    def wait(self, index, arrives):
        place = self.all_ref.at[index]
        put(
            place, place, self.send_sem.at[0], self.recv_sem.at[arrives], self.to["near"]
        ).wait_recv()

    ARRIVES = ("z", "down", "up", "z down", "z up", "far", "z far")

    def arrived(self, name):
        self.wait(self.piece[name], self.ARRIVES.index(name))
        self.send_near(name)

    def send_near(self, name):
        self.send(name, "near", 7 + list(self.piece).index(name))

    def step(self, s):
        if s == 0:
            self.own.wait()
            for copy in self.fetches:
                copy.wait()
            self.send("own", "z", 0)
            self.send("own", "up", 1)
            self.send("own", "down", 2)
            self.send_near("own")
        if s == 1:
            self.arrived("z")
            self.send("z", "up", 3)
            self.send("z", "down", 4)
        if s == 2:
            self.arrived("down")
            self.send("down", "up", 5)
            self.arrived("up")
        if s == 3:
            self.arrived("z up")
            self.send("z up", "down", 6)
            self.arrived("z down")
            self.arrived("far")

    def last(self):
        self.arrived("z far")

    def end(self):
        for i, name in enumerate(self.piece):
            self.wait(self.near_piece[name], 7 + i)
        for copy in self.started:
            copy.wait_send()


class Shared:
    def __init__(self, own, kv_ref, own_sem, send_sem, recv_sem, near_send, near_recv, along_send):
        per = lax.axis_size("ctx") // 2
        ctx = lax.axis_index("ctx")
        self.per = per
        self.core = lax.rem(ctx, 2)
        self.chip = lax.axis_index("dp") * per + lax.div(ctx, 2)
        self.chips = lax.axis_size("dp") * per
        self.block = self.chip * 2 + self.core
        self.sibling = {"ctx": ctx + 1 - 2 * self.core}
        self.sibling_block = self.block + 1 - 2 * self.core
        self.own, self.kv_ref, self.own_sem = own, kv_ref, own_sem
        self.send_sem, self.recv_sem = send_sem, recv_sem
        self.near_send, self.near_recv = near_send, near_recv
        self.along_send = along_send
        self.x = lax.rem(self.chip, per)

    def run(self, ref, s):
        first, last = (CUTS[cut] for cut in BATCHES[s])
        return ref.at[pl.ds(first, last - first)]

    def to_chip(self, k, s):
        other = self.chip + k
        return put(
            self.run(self.own, s),
            self.run(self.kv_ref.at[self.block], s),
            self.send_sem.at[k - 1, s],
            self.recv_sem.at[k - 1, s],
            {"dp": lax.div(other, self.per), "ctx": lax.rem(other, self.per) * 2 + self.core},
        )

    def to_sibling(self, k, s):
        place = self.run(self.kv_ref.at[self.block - 2 * k], s)
        return put(
            self.run(self.own, s) if k == 0 else place,
            place,
            self.near_send.at[k, s],
            self.near_recv.at[k, s],
            self.sibling,
        )

    def keep(self, s):
        return pltpu.make_async_copy(
            self.run(self.own, s), self.run(self.kv_ref.at[self.block], s), self.own_sem.at[s]
        )

    def sends(self, act):
        for k in (2, 1, 3):

            @pl.when(self.x + k < self.per)
            def _(k=k):
                act(k)

        @pl.when(self.chip + self.per < self.chips)
        def _():
            act(self.per)

    def send(self, s):
        self.sends(lambda k: self.to_chip(k, s).start())
        self.to_sibling(0, s).start()
        self.keep(s).start()

    def along(self, m, s):
        place = self.run(self.kv_ref.at[self.block - 2 * self.per], s)
        return put(
            place,
            place,
            self.along_send.at[m - 1, s],
            self.recv_sem.at[self.per - m - 1, s],
            {"ctx": (self.x - m) * 2 + self.core},
        )

    def relays(self, act):
        for m in (2, 1, 3):

            @pl.when((self.chip >= self.per) & (self.x >= m))
            def _(m=m):
                act(m)

    def pass_on(self, s):
        for k in (4, 1, 3, 2):

            @pl.when(self.chip - k >= 0)
            def _(k=k):
                place = self.run(self.kv_ref.at[self.block - 2 * k], s)
                put(
                    place,
                    place,
                    self.send_sem.at[k - 1, s],
                    self.recv_sem.at[k - 1, s],
                    self.sibling,
                ).wait_recv()

            if k == self.per:
                self.relays(lambda m: self.along(m, s).start())

            @pl.when(self.chip - k >= 0)
            def _(k=k):
                self.to_sibling(k, s).start()

    def from_sibling(self, k, s):
        place = self.run(self.kv_ref.at[self.sibling_block - 2 * k], s)
        put(
            place, place, self.near_send.at[k, s], self.near_recv.at[k, s], self.sibling
        ).wait_recv()

    def end(self):
        for s in range(len(BATCHES)):
            self.keep(s).wait()
            self.to_sibling(0, s).wait_send()
            self.from_sibling(0, s)
        for k in range(1, SEEN_CHIPS + 1):

            @pl.when(self.chip - k >= 0)
            def _(k=k):
                for s in range(len(BATCHES)):
                    self.to_sibling(k, s).wait_send()
                    self.from_sibling(k, s)

        for s in range(len(BATCHES)):
            self.sends(lambda k, s=s: self.to_chip(k, s).wait_send())
            self.relays(lambda m, s=s: self.along(m, s).wait_send())


def project_kernel(
    tok_hbm,
    gain_hbm,
    source_hbm,
    segment_hbm,
    w_ref,
    bias_hbm,
    freq_hbm,
    wo_ref,
    q_ref,
    spots_ref,
    kv_ref,
    columns_ref,
    tok,
    gain_rows,
    sources_row,
    segments_row,
    bias_row,
    freq_row,
    stats,
    docs,
    scales,
    cosines,
    sines,
    normed,
    buf,
    w_buf,
    total,
    own,
    load_sem,
    w_sem,
    stat_send,
    stat_recv,
    doc_send,
    doc_recv,
    gather_send,
    gather_recv,
    a2a_send,
    a2a_recv,
    col_send,
    col_recv,
    col_own,
    kv_own,
    kv_send,
    kv_recv,
    near_send,
    near_recv,
    along_send,
):
    me = lax.axis_index("tensor")
    replica = lax.axis_index("dp") * lax.axis_size("ctx") + lax.axis_index("ctx")
    replicas = docs.shape[0]
    rows, width = tok.shape
    features = width * N_T
    step = rows // SUBS
    others = all_others(me)
    alike = [ring_of(lax.rem(replica + d, replicas)) for d in range(1, replicas)]
    greet(others)
    for other in alike:
        pl.semaphore_signal(
            pltpu.get_barrier_semaphore(), inc=1, device_id=other, device_id_type=MESH
        )
    small = []
    for i, (src, dst) in enumerate(
        (
            (source_hbm, sources_row),
            (segment_hbm, segments_row),
            (gain_hbm, gain_rows),
            (bias_hbm, bias_row),
            (freq_hbm, freq_row),
        )
    ):
        small.append(pltpu.make_async_copy(src, dst, load_sem.at[SUBS + i]))
        small[-1].start()
    token_loads = []
    for i in range(SUBS):
        cut = pl.ds(i * step, step)
        token_loads.append(pltpu.make_async_copy(tok_hbm.at[cut], tok.at[cut], load_sem.at[i]))
        token_loads[-1].start()

    def run_of(ref, s):
        return ref.at[pl.ds(CUTS[s], CUTS[s + 1] - CUTS[s])]

    gather = Gather(tok, buf, run_of, gather_send, gather_recv, OVER_Z)
    w_loads = []
    for i, t in enumerate([me] + gather.owner):
        w_loads.append(
            pltpu.make_async_copy(
                w_ref.at[pl.ds(pl.multiple_of(t * width, width), width)], w_buf.at[i], w_sem.at[i]
            )
        )
        w_loads[-1].start()

    for copy in small:
        copy.wait()
    sources = sources_row[...]
    segments = segments_row[...]
    row = replica * rows + lax.broadcasted_iota(jnp.int32, (1, rows), 1)
    none = rows * replicas
    lane = lax.broadcasted_iota(jnp.int32, (8, 128), 1)
    line = lax.broadcasted_iota(jnp.int32, (8, 128), 0)
    table = jnp.full((8, 128), none, jnp.int32)
    for doc in range(DOC_IDS):
        of_doc = segments == doc
        first_source = jnp.min(jnp.where(of_doc, sources, none), axis=1, keepdims=True)
        first_packed = jnp.min(jnp.where(of_doc, row, none), axis=1, keepdims=True)
        found = jnp.where(line == 0, first_source, first_packed)
        table = jnp.where(lane == doc, found, table)
    docs[pl.ds(replica, 1)] = table[None]
    for i in range(SUBS):
        token_loads[i].wait()
        squares = jnp.zeros((step, 128), jnp.float32)
        for j in range(width // 128):
            part = tok[i * step : (i + 1) * step, j * 128 : (j + 1) * 128].astype(jnp.float32)
            squares = squares + part * part
        summed = jnp.sum(squares.T, axis=0, keepdims=True)
        stats[pl.ds(me, 1), :, i * step : (i + 1) * step] = jnp.broadcast_to(
            summed[None], (1, 8, step)
        )
    greeted(N_T - 1 + replicas - 1)

    stat_copies = []
    for d, other in enumerate(others):
        stat_copies.append(
            remote(stats.at[me], stats.at[me], stat_send.at[d], stat_recv.at[d], other)
        )
        stat_copies[-1].start()
    doc_copies = []
    for d, other in enumerate(alike):
        place = docs.at[replica]
        doc_copies.append(put(place, place, doc_send.at[d], doc_recv.at[d], other))
        doc_copies[-1].start()
    for s in range(DEPTH):
        gather.send_own(s)
    columns = Columns(wo_ref, columns_ref, a2a_send, a2a_recv, col_send, col_recv, col_own)
    columns.fetch()
    for copy in stat_copies:
        copy.wait()
    summed = stats[0]
    for t in range(1, N_T):
        summed = summed + stats[t]
    scale = lax.rsqrt(summed[0:1] * (1.0 / features) + 1e-06)
    for i in range(SUBS):
        here = slice(i * step, (i + 1) * step)
        scales[here, :] = jnp.broadcast_to(scale[:, here], (128, step)).T

    shared = Shared(own, kv_ref, kv_own, kv_send, kv_recv, near_send, near_recv, along_send)
    def find_spots():
        for copy in doc_copies:
            copy.wait()
        table = docs[0]
        for r in range(1, replicas):
            table = jnp.minimum(table, docs[r])
        start = jnp.full((1, rows), -1, jnp.int32)
        place = row
        for doc in range(DOC_IDS):
            first_source = table[0:1, doc : doc + 1]
            first_packed = table[1:2, doc : doc + 1]
            later = (first_source <= row) & (first_source > start)
            start = jnp.where(later, first_source, start)
            place = jnp.where(later, row + (first_packed - first_source), place)
        spots_ref[...] = jnp.where(
            lax.broadcasted_iota(jnp.int32, (8, rows), 0) == 0, start, place
        )
        position = lax.rem(place, PACK).astype(jnp.float32)
        first = lax.broadcasted_iota(jnp.int32, (step, HD), 1) < HD // 2
        for i in range(SUBS):
            here = slice(i * step, (i + 1) * step)
            angle = jnp.broadcast_to(position[:, here], (128, step)).T * freq_row[...]
            cosines[here, :] = jnp.cos(angle)
            sine = jnp.sin(angle)
            sines[here, :] = jnp.where(first, -sine, sine)

    def use(kind, s):
        i = kind + 1
        if s == 0:
            w_loads[i].wait()
        owner = me if kind < 0 else gather.owner[kind]
        chunk = tok if kind < 0 else buf.at[owner]
        here = slice(CUTS[s], CUTS[s + 1])
        along = scales[here, :]
        for j in range(width // 128):
            cut = slice(j * 128, (j + 1) * 128)
            wide = chunk[here, cut].astype(jnp.float32)
            normed[here, cut] = (wide * along * gain_rows[owner, :, cut]).astype(jnp.bfloat16)
        term = jnp.dot(normed[here, :], w_buf[i], preferred_element_type=jnp.float32)
        if kind < 0:
            total[here, :] = term
        else:
            total[here, :] += term

    def done(s):
        here = slice(CUTS[s], CUTS[s + 1])
        bias = bias_row[...].astype(jnp.float32)
        cosine = cosines[here, :]
        sine = sines[here, :]

        def slot(index):
            cut = slice(index * HD, (index + 1) * HD)
            return (total[here, cut] + bias[:, cut]).astype(jnp.bfloat16)

        def turned(index):
            wide = slot(index).astype(jnp.float32)
            return (wide * cosine + pltpu.roll(wide, HD // 2, 1) * sine).astype(jnp.bfloat16)

        own[here, :HD] = turned(GROUP)
        own[here, HD:] = slot(GROUP + 1)
        for batch, (_, end) in enumerate(BATCHES):
            if end == s + 1:
                shared.send(batch)
        for head in range(GROUP):
            q_ref[here, head * HD : (head + 1) * HD] = turned(head)

    find_spots()
    gather.run(use, done, columns.step)
    shared.pass_on(0)
    shared.pass_on(1)
    columns.last()
    shared.pass_on(2)
    columns.end()
    shared.end()
    gather.end()


def project(tokens, gain, sources, segments, weight, bias, out_weight, replicas):
    rows, width = tokens.shape
    columns = weight.shape[1]
    depth, out_width = out_weight.shape
    half = HD // 2
    freqs = (1e6 ** (-(np.arange(half) * 2.0) / HD)).astype(np.float32)
    freqs = jnp.asarray(np.concatenate([freqs, freqs])[None])
    hbm = pl.BlockSpec(memory_space=pltpu.HBM)
    vmem = pl.BlockSpec(memory_space=VMEM)
    return pl.pallas_call(
        project_kernel,
        out_shape=(
            jax.ShapeDtypeStruct((rows, GROUP * HD), jnp.bfloat16),
            jax.ShapeDtypeStruct((8, rows), jnp.int32),
            jax.ShapeDtypeStruct((replicas, rows, 2 * HD), jnp.bfloat16),
            jax.ShapeDtypeStruct((replicas, N_T, depth // replicas, out_width // N_T), jnp.bfloat16),
        ),
        in_specs=[hbm] * 8,
        out_specs=(vmem, vmem, hbm, hbm),
        scratch_shapes=[
            VMEM((rows, width), jnp.bfloat16),
            VMEM((N_T, 1, width), jnp.float32),
            VMEM((1, rows), jnp.int32),
            VMEM((1, rows), jnp.int32),
            VMEM((1, columns), jnp.bfloat16),
            VMEM((1, HD), jnp.float32),
            VMEM((N_T, 8, rows), jnp.float32),
            VMEM((replicas, 8, 128), jnp.int32),
            VMEM((rows, HD), jnp.float32),
            VMEM((rows, HD), jnp.float32),
            VMEM((rows, HD), jnp.float32),
            VMEM((rows, width), jnp.bfloat16),
            VMEM((N_T, rows, width), jnp.bfloat16),
            VMEM((N_T, width, columns), jnp.bfloat16),
            VMEM((rows, columns), jnp.float32),
            VMEM((rows, 2 * HD), jnp.bfloat16),
            DMA((SUBS + 5,)),
            DMA((N_T,)),
            DMA((N_T - 1,)),
            DMA((N_T - 1,)),
            DMA((replicas - 1,)),
            DMA((replicas - 1,)),
            *GATHER_SEMS,
            DMA((N_T - 1,)),
            DMA((N_T - 1,)),
            DMA((15,)),
            DMA((15,)),
            DMA,
            DMA((len(BATCHES),)),
            DMA((SEEN_CHIPS, len(BATCHES))),
            DMA((SEEN_CHIPS, len(BATCHES))),
            DMA((SEEN_CHIPS + 1, len(BATCHES))),
            DMA((SEEN_CHIPS + 1, len(BATCHES))),
            DMA((SEEN_CHIPS - 1, len(BATCHES))),
        ],
        compiler_params=pltpu.CompilerParams(
            collective_id=1, has_side_effects=True, vmem_limit_bytes=58 * 2**20
        ),
        cost_estimate=pl.CostEstimate(
            flops=2 * rows * width * N_T * columns, bytes_accessed=10**8, transcendentals=10**5
        ),
    )(
        tokens,
        gain.reshape(N_T, 1, width),
        sources.reshape(1, rows),
        segments.reshape(1, rows),
        weight,
        bias,
        freqs,
        out_weight,
    )


def output_kernel(
    own_hbm,
    w_ref,
    out_ref,
    own_ref,
    buf,
    w_buf,
    total,
    ready,
    gather_send,
    gather_recv,
    w_sem,
    out_send,
    out_recv,
    own_sem,
):
    me = lax.axis_index("tensor")
    part = own_ref.shape[1] // SUBS
    others = all_others(me)
    greet(others)
    load_own = pltpu.make_async_copy(own_hbm, own_ref, own_sem.at[SUBS])
    load_own.start()

    def run_of(ref, s):
        return ref.at[:, pl.ds(s * part, part)]

    gather = Gather(own_ref, buf, run_of, gather_send, gather_recv, OUT_OVER_Z)
    loads = []
    for i, t in enumerate([me] + gather.owner):
        loads.append(pltpu.make_async_copy(w_ref.at[:, t], w_buf.at[i], w_sem.at[i]))
        loads[-1].start()
    load_own.wait()
    greeted(N_T - 1)
    depth = own_ref.shape[2]
    columns = total.shape[1]
    place = pl.ds(pl.multiple_of(me * columns, columns), columns)
    copies = []

    def use(kind, s):
        i = kind + 1
        if s == 0:
            loads[i].wait()
        chunk = own_ref if kind < 0 else buf.at[gather.owner[kind]]
        weight = w_buf[i].reshape(depth, columns)
        rows = chunk[:, s * part : (s + 1) * part, :].reshape(N_T * part, depth)
        term = jnp.dot(rows, weight, preferred_element_type=jnp.float32)
        term = term.astype(jnp.bfloat16).astype(jnp.float32)
        here = slice(s * N_T * part, (s + 1) * N_T * part)
        if kind < 0:
            total[here, :] = term
        else:
            total[here, :] += term

    def done(s):
        here = slice(s * N_T * part, (s + 1) * N_T * part)
        ready[s] = total[here, :].astype(jnp.bfloat16).reshape(N_T, part, columns)
        target = out_ref.at[pl.ds(s * part, part), place]
        for d, other in enumerate(others):
            copies.append(
                remote(ready.at[s, other], target, out_send.at[d, s], out_recv.at[d, s], other)
            )
            copies[-1].start()
        copies.append(pltpu.make_async_copy(ready.at[s, me], target, own_sem.at[s]))
        copies[-1].start()

    for s in range(DEPTH):
        gather.send_own(s)
    gather.run(use, done, lambda s: None)
    for copy in copies:
        copy.wait()
    gather.end()


def project_out(attended, weight):
    rows, depth = attended.shape
    columns = weight.shape[3]
    each = rows // N_T
    return pl.pallas_call(
        output_kernel,
        out_shape=jax.ShapeDtypeStruct((each, columns * N_T), jnp.bfloat16),
        in_specs=[pl.BlockSpec(memory_space=pltpu.HBM), pl.BlockSpec(memory_space=pltpu.HBM)],
        out_specs=pl.BlockSpec(memory_space=pltpu.HBM),
        scratch_shapes=[
            VMEM((N_T, each, depth), jnp.bfloat16),
            VMEM((N_T, N_T, each, depth), jnp.bfloat16),
            VMEM((N_T, weight.shape[0], weight.shape[2], columns), jnp.bfloat16),
            VMEM((rows, columns), jnp.float32),
            VMEM((SUBS, N_T, each // SUBS, columns), jnp.bfloat16),
            *GATHER_SEMS,
            DMA((N_T,)),
            DMA((N_T - 1, SUBS)),
            DMA((N_T - 1, SUBS)),
            DMA((SUBS + 1,)),
        ],
        compiler_params=pltpu.CompilerParams(
            collective_id=3, has_side_effects=True, vmem_limit_bytes=48 * 2**20
        ),
        cost_estimate=pl.CostEstimate(
            flops=2 * rows * depth * N_T * columns, bytes_accessed=10**8, transcendentals=0
        ),
    )(attended.reshape(N_T, each, depth), weight)


TILE_Q = 256
SEEN_BLOCKS = 2 * SEEN_CHIPS
TILE_K = 256
LOW = -1e30


def attend_kernel(
    spots_hbm, q_hbm, kv_hbm, out_ref, starts, spots_ref, q_ref, kv_ref, load_sem, kv_sem
):
    rows = q_ref.shape[0]
    block = lax.axis_index("dp") * lax.axis_size("ctx") + lax.axis_index("ctx")
    first_row = block * rows
    loads = [
        pltpu.make_async_copy(spots_hbm, starts, load_sem.at[0]),
        pltpu.make_async_copy(spots_hbm, spots_ref, load_sem.at[1]),
        pltpu.make_async_copy(q_hbm, q_ref, load_sem.at[2]),
    ]
    for load in loads:
        load.start()

    def kv_load(back):
        return pltpu.make_async_copy(
            kv_hbm.at[block - back],
            kv_ref.at[pl.ds(pl.multiple_of((block - back) * rows, rows), rows)],
            kv_sem.at[back],
        )

    for back in range(SEEN_BLOCKS + 1):

        @pl.when(block - back >= 0)
        def _(back=back):
            kv_load(back).start()

    for load in loads:
        load.wait()
    for back in range(SEEN_BLOCKS + 1):

        @pl.when(block - back >= 0)
        def _(back=back):
            kv_load(back).wait()

    heads = q_ref.shape[1] // HD
    factor = HD**-0.5 * 1.4426950408889634
    for a in range(rows // TILE_Q):
        base = first_row + a * TILE_Q
        start = spots_ref[0:1, a * TILE_Q : (a + 1) * TILE_Q]
        query_row = base + lax.broadcasted_iota(jnp.int32, (1, TILE_Q), 1)
        low_tile = lax.div(starts[0, a * TILE_Q], TILE_K)
        high_tile = lax.div(base + TILE_Q, TILE_K)

        def one(tile, carry, masked, a=a, start=start, query_row=query_row):
            cut = pl.ds(pl.multiple_of(tile * TILE_K, TILE_K), TILE_K)
            keys = kv_ref[cut, :HD]
            values = kv_ref[cut, HD:].T
            if masked:
                key_row = tile * TILE_K + lax.broadcasted_iota(jnp.int32, (TILE_K, TILE_Q), 0)
                allowed = (key_row >= start) & (key_row <= query_row)
            after = []
            for h in range(heads):
                top, denominator, weighted = carry[h]
                query = q_ref[a * TILE_Q : (a + 1) * TILE_Q, h * HD : (h + 1) * HD]
                scores = lax.dot_general(
                    keys, query, (((1,), (1,)), ((), ())), preferred_element_type=jnp.float32
                )
                scores = scores * factor
                if masked:
                    scores = jnp.where(allowed, scores, 2 * LOW)
                new_top = jnp.maximum(top, jnp.max(scores, axis=0, keepdims=True))
                weights = jnp.exp2(scores - new_top)
                shrink = jnp.exp2(top - new_top)
                denominator = denominator * shrink + jnp.sum(weights, axis=0, keepdims=True)
                coarse = weights.astype(jnp.bfloat16)
                fine = (weights - coarse.astype(jnp.float32)).astype(jnp.bfloat16)
                weighted = weighted * shrink
                weighted += jnp.dot(values, coarse, preferred_element_type=jnp.float32)
                weighted += jnp.dot(values, fine, preferred_element_type=jnp.float32)
                after.append((new_top, denominator, weighted))
            return tuple(after)

        full_tile = jnp.minimum(
            lax.div(starts[0, (a + 1) * TILE_Q - 1] + TILE_K - 1, TILE_K), high_tile - 1
        )
        begin = (
            jnp.full((1, TILE_Q), LOW, jnp.float32),
            jnp.zeros((1, TILE_Q), jnp.float32),
            jnp.zeros((HD, TILE_Q), jnp.float32),
        )
        ended = one(high_tile - 1, (begin,) * heads, True)
        ended = lax.fori_loop(
            full_tile, high_tile - 1, lambda t, carry: one(t, carry, False), ended
        )
        ended = lax.fori_loop(low_tile, full_tile, lambda t, carry: one(t, carry, True), ended)
        for h in range(heads):
            _, denominator, weighted = ended[h]
            out_ref[a * TILE_Q : (a + 1) * TILE_Q, h * HD : (h + 1) * HD] = (
                (weighted / denominator).T.astype(jnp.bfloat16)
            )


def attend(spots, queries, both):
    blocks, rows, width = both.shape
    hbm = pl.BlockSpec(memory_space=pltpu.HBM)
    return pl.pallas_call(
        attend_kernel,
        out_shape=jax.ShapeDtypeStruct(queries.shape, jnp.bfloat16),
        in_specs=[hbm, hbm, hbm],
        out_specs=pl.BlockSpec(memory_space=VMEM),
        scratch_shapes=[
            pltpu.SMEM(spots.shape, jnp.int32),
            VMEM(spots.shape, jnp.int32),
            VMEM(queries.shape, jnp.bfloat16),
            VMEM((blocks * rows, width), jnp.bfloat16),
            DMA((3,)),
            DMA((SEEN_BLOCKS + 1,)),
        ],
        compiler_params=pltpu.CompilerParams(vmem_limit_bytes=58 * 2**20),
        cost_estimate=pl.CostEstimate(flops=10**9, bytes_accessed=10**7, transcendentals=10**7),
    )(spots, queries, both)


def per_device(
    tokens, norm_gain, project_weight, project_bias, output_weight, source_row, segment_id
):
    replicas = lax.axis_size("dp") * lax.axis_size("ctx")
    flat_weight = project_weight.reshape(project_weight.shape[0], -1)
    queries, spots, both, out_columns = project(
        tokens, norm_gain, source_row, segment_id, flat_weight, project_bias, output_weight, replicas
    )
    attended = attend(spots, queries, both)
    return project_out(attended, out_columns)


def solution(mesh):
    placed = (
        P(("dp", "ctx"), "tensor"),
        P(),
        P(None, "tensor", None),
        P("tensor", None),
        P("tensor", None),
        P(("dp", "ctx")),
        P(("dp", "ctx")),
    )
    return jax.shard_map(
        per_device,
        mesh=mesh,
        in_specs=placed,
        out_specs=P(("dp", "ctx", "tensor"), None),
        check_vma=False,
    )
```
